32 devices in a mesh: req: 16 (over z, y, x), col: 2 (over core).
Axes of the slice: x: 2, y: 2, z: 4, core: 2. Of those that a mesh axis runs over, the one named last changes fastest.
Arguments:
- tokens: bfloat16 [8192, 1024], P(('req', 'col')), may hold values from -6 to 6
- norm_gain_pair: float32 [2, 1024], replicated, may hold values from 0.5 to 1.5
- query_key_value_weight: bfloat16 [3, 1024, 1024], P(None, None, 'col'), may hold values from -1 to 1
- head_gate_weight: bfloat16 [2, 1024, 8], P(None, None, 'col'), may hold values from -0.1875 to 0.1875
- decay_logit_bias: float32 [8], P('col'), may hold values from -1 to 1024, as said below
- adapter_down_factor: bfloat16 [64, 1024, 16], P('col'), may hold values from -0.1875 to 0.1875
- adapter_up_factor: bfloat16 [64, 16, 1024], P(None, None, 'col'), may hold values from -1.5 to 1.5
- lengths: int32 [16, 2, 3], P('req'), may hold values from 1 to 128, 256 in all within a row
- request_adapter_index: int32 [16, 6], P('req'), may hold values from 0 to 63
- request_cache_index: int32 [16, 6], P('req'), may hold values from 0 to 127
- caches: bfloat16 [64, 8, 128, 128], P('req', 'col'), may hold values from -6 to 6
- head_output_weight: bfloat16 [1024, 1024], P('col'), may hold values from -0.1875 to 0.1875
- feedforward_weight: bfloat16 [3, 1024, 2816], P(None, None, 'col'), may hold values from -0.1875 to 0.1875
Outputs:
- layer_out: bfloat16 [8192, 1024], P(('req', 'col'))
The draws below stay inside these ranges and needn't reach their ends.
Inputs may be any that keep to these rules, and one draw needn't show every extreme that they name: The 3 lengths of one device sum to 256, and the longest of them is exactly 128. `request_cache_index`: a value of 64 or more means that the request has no cached memory state. `decay_logit_bias`: at most the logarithm of 512.
All inputs are finite; a program needn't handle non-finite values.
Results may differ from the reference program's by a relative error of at most 0.015.
Values may be sent and summed in bfloat16 or wider, within the bound.
A program may use at most 192 MiB of HBM per device.

```python
import math
import jax
import jax.numpy as jnp
import numpy as np
from jax import lax

MODEL_WIDTH = 1024
H = 8
DH = 128
FF = 2816
ADAPTER_RANK = 16
ADAPTER_TOTAL = 64
TOK_DEV = 256
SEQ_DEV = 3
SEQS = 6
TOK_GRP = 512
MOST = 128
TOKENS = 8192
CACHES = 64
N_REQ = 16
N_COL = 2


def draw_query_key_value_weight(key, part):
    base_key = jax.random.fold_in(key, 11)
    normal_key = jax.random.fold_in(base_key, 0)
    weights = jax.random.truncated_normal(normal_key, -4.0, 4.0, (3, MODEL_WIDTH, MODEL_WIDTH), jnp.float32) * (1.0 / math.sqrt(MODEL_WIDTH))
    return weights.astype(jnp.bfloat16)


def draw_decay_logit_bias(key, part):
    base_key = jax.random.fold_in(key, 23)
    top = math.log(4.0 * MOST)
    values = jax.random.uniform(base_key, (H,), jnp.float32, -1.0, top)
    return values.astype(jnp.float32)


def place_ends(values, own_key, low, top_value):
    index_at = [jax.random.randint(jax.random.fold_in(own_key, axis), (), 0, length) for axis, length in enumerate(values.shape)]
    longest = values.shape.index(max(values.shape))
    next_to = index_at[:longest] + [(index_at[longest] + 1) % values.shape[longest]] + index_at[longest + 1:]
    return values.at[tuple(index_at)].set(low).at[tuple(next_to)].set(top_value)


def steps_of(stream_key, extent, shards, low, largest):
    def one(position, parts):
        steps = jax.random.uniform(jax.random.fold_in(jax.random.fold_in(stream_key, 6), position), (parts,), jnp.float32, low / len(shards), largest / len(shards))
        return jnp.repeat(jnp.exp(steps), extent[position] // parts).reshape((-1,) + (1,) * (len(extent) - position - 1))

    factor_of = one(*shards[0])
    for cut in shards[1:]:
        factor_of = factor_of * one(*cut)
    return factor_of


def profile(number_of, total, bound, lean):
    weights = [(1 << 20) // math.isqrt(rank ** lean) + 1 for rank in range(2, number_of + 1)]
    rest, given = total - bound - (number_of - 1), [1] * (number_of - 1)
    while rest > 0:
        free = [i for i in range(number_of - 1) if given[i] < bound]
        whole, budget = sum([weights[i] for i in free]), rest
        for i in free:
            extra = min(bound - given[i], max(1, budget * weights[i] // whole), rest)
            given[i] = given[i] + extra
            rest = rest - extra
    return np.array([bound] + given)


def uneven_parts(rng, amount, total, limit, slope):
    if amount == 2:
        one = jax.random.randint(rng, (), max(1, total - limit), min(limit, total - 1) + 1)
        return jnp.stack([one, total - one])
    sizes = jnp.asarray(profile(amount, total, limit, slope), jnp.int32)
    couples = (amount - 1) // 2
    giver, receiver = sizes[1:1 + 2 * couples:2], sizes[2:2 + 2 * couples:2]
    room = jnp.minimum(giver - 1, limit - receiver)
    shifted = jax.random.randint(jax.random.fold_in(rng, 1), (couples,), 0, 1 << 20) % (room + 1)
    sizes = sizes.at[1:1 + 2 * couples:2].set(giver - shifted).at[2:2 + 2 * couples:2].set(receiver + shifted)
    return sizes[jax.random.permutation(jax.random.fold_in(rng, 2), amount)]


def scatter_about(stream_key, dims, deviation, limit, shards=(), kind=jnp.bfloat16):
    level = steps_of(stream_key, dims, shards, -0.22, 0.18) if shards else 1.0
    values = jax.random.normal(stream_key, dims, jnp.float32) * deviation * level
    return jnp.minimum(jnp.maximum(values, -limit), limit).astype(kind)


def setup_inputs(seed: int = 0) -> dict:
    arg_keys = jax.random.split(jax.random.key(seed), 14)
    return {
        "tokens": scatter_about(arg_keys[0], (TOKENS, MODEL_WIDTH), 1.0, 6.0, ((0, 32),)),
        "norm_gain_pair": jnp.clip(1.0 + 0.1 * jax.random.normal(arg_keys[1], (2, MODEL_WIDTH), jnp.float32), 0.5, 1.5),
        "query_key_value_weight": draw_query_key_value_weight(jax.random.fold_in(arg_keys[13], 71), 0),
        "head_gate_weight": scatter_about(arg_keys[3], (2, MODEL_WIDTH, H), MODEL_WIDTH ** -0.5, 0.1875, ((2, 2),)),
        "decay_logit_bias": draw_decay_logit_bias(jax.random.fold_in(arg_keys[13], 71), 0),
        "adapter_down_factor": scatter_about(arg_keys[5], (ADAPTER_TOTAL, MODEL_WIDTH, ADAPTER_RANK), MODEL_WIDTH ** -0.5, 0.1875, ((0, 2),)),
        "adapter_up_factor": scatter_about(arg_keys[6], (ADAPTER_TOTAL, ADAPTER_RANK, MODEL_WIDTH), ADAPTER_RANK ** -0.5, 1.5, ((2, 2),)),
        "lengths": jax.vmap(lambda own: uneven_parts(own, SEQ_DEV, TOK_DEV, MOST, 2))(jax.random.split(arg_keys[7], N_REQ * N_COL)).reshape((N_REQ, N_COL, SEQ_DEV)).astype(jnp.int32),
        "request_adapter_index": place_ends(jax.random.randint(arg_keys[8], (N_REQ, SEQS), 0, ADAPTER_TOTAL), jax.random.fold_in(arg_keys[8], 1), 0, ADAPTER_TOTAL - 1).astype(jnp.int32),
        "request_cache_index": place_ends(jax.random.randint(arg_keys[9], (N_REQ, SEQS), 0, 2 * CACHES), jax.random.fold_in(arg_keys[9], 1), 0, (2 * CACHES) - 1).astype(jnp.int32),
        "caches": scatter_about(arg_keys[10], (CACHES, H, DH, DH), 1.0, 6.0, ((0, 16), (1, 2))),
        "head_output_weight": scatter_about(arg_keys[11], (MODEL_WIDTH, MODEL_WIDTH), MODEL_WIDTH ** -0.5, 0.1875, ((0, 2),)),
        "feedforward_weight": scatter_about(arg_keys[12], (3, MODEL_WIDTH, FF), MODEL_WIDTH ** -0.5, 0.1875, ((2, 2),)),
    }


epsilon = 1e-05

def rms_scale(values, gain):
    widened = values.astype(jnp.float32)
    factor = lax.rsqrt(lax.optimization_barrier(jnp.mean(widened * widened, axis=-1, keepdims=True)) + epsilon)
    return (widened * factor * gain).astype(jnp.bfloat16)

def reference(tokens, norm_gain_pair, query_key_value_weight, head_gate_weight, decay_logit_bias, adapter_down_factor, adapter_up_factor, lengths, request_adapter_index, request_cache_index, caches, head_output_weight, feedforward_weight):
    scale = 1.0 / math.sqrt(DH)

    def group_layer(inputs):
        group_rows, nested_lengths, grouped_adapter_rows, group_caches = inputs
        group_lengths = nested_lengths.reshape(SEQS).astype(jnp.int32)
        count = group_rows.shape[0]
        normalized_rows = rms_scale(group_rows, norm_gain_pair[0])
        positions = jnp.arange(count, dtype=jnp.int32)
        ends = jnp.cumsum(group_lengths).astype(jnp.int32)
        starts = (ends - group_lengths).astype(jnp.int32)
        member = ((positions[:, None] >= starts[None, :]) & (positions[:, None] < ends[None, :])).astype(jnp.float32)
        segment = lax.optimization_barrier(jnp.sum((positions[:, None] >= ends[None, :]).astype(jnp.int32), axis=1))
        proj_q = jnp.dot(normalized_rows, query_key_value_weight[0], preferred_element_type=jnp.float32)
        proj_k = jnp.dot(normalized_rows, query_key_value_weight[1], preferred_element_type=jnp.float32)
        proj_v = jnp.dot(normalized_rows, query_key_value_weight[2], preferred_element_type=jnp.float32)
        low_rank_delta = jnp.zeros((count, ADAPTER_RANK), jnp.float32)
        for request_number in range(SEQS):
            adapter_term = jnp.dot(normalized_rows, adapter_down_factor[grouped_adapter_rows[request_number]], preferred_element_type=jnp.float32)
            low_rank_delta = low_rank_delta + member[:, request_number:request_number + 1] * adapter_term
        low_rank_delta = low_rank_delta.astype(jnp.bfloat16)
        delta = jnp.zeros((count, MODEL_WIDTH), jnp.float32)
        for request_number in range(SEQS):
            adapter_term = jnp.dot(low_rank_delta, adapter_up_factor[grouped_adapter_rows[request_number]], preferred_element_type=jnp.float32)
            delta = delta + member[:, request_number:request_number + 1] * adapter_term
        queries = (proj_q + delta).astype(jnp.bfloat16)
        keys = proj_k.astype(jnp.bfloat16)
        values = proj_v.astype(jnp.bfloat16)
        log_keep = jax.nn.log_sigmoid(jnp.dot(normalized_rows, head_gate_weight[0], preferred_element_type=jnp.float32) + decay_logit_bias[None, :])
        mix_gate = jax.nn.sigmoid(jnp.dot(normalized_rows, head_gate_weight[1], preferred_element_type=jnp.float32))
        running = jnp.cumsum(log_keep, axis=0)
        before = running - log_keep
        start_level = before[starts]
        level = running - lax.optimization_barrier(jnp.sum(member[:, :, None] * start_level[None, :, :], axis=1))
        states = []
        for request_number in range(SEQS):
            ident = group_caches[request_number]
            picked = caches[jnp.minimum(ident, CACHES - 1)]
            states.append(jnp.where(ident < CACHES, picked, jnp.zeros_like(picked)))
        allowed = (segment[:, None] == segment[None, :]) & (positions[None, :] <= positions[:, None])
        outputs = []
        for head in range(H):
            cols = slice(head * DH, (head + 1) * DH)
            q_head = queries[:, cols]
            k_head = keys[:, cols]
            v_head = values[:, cols]
            scores = jnp.dot(q_head, k_head.T, preferred_element_type=jnp.float32) * scale
            masked = jnp.where(allowed, scores, -jnp.inf)
            peak = lax.optimization_barrier(jnp.max(masked, axis=1, keepdims=True))
            weights = jnp.exp(masked - peak)
            probs = (weights / lax.optimization_barrier(jnp.sum(weights, axis=1, keepdims=True))).astype(jnp.bfloat16)
            attended = jnp.dot(probs, v_head, preferred_element_type=jnp.float32)
            gap = jnp.where(allowed, running[:, head][:, None] - running[:, head][None, :], -jnp.inf)
            memory_w = (scores * jnp.exp(gap)).astype(jnp.bfloat16)
            intra = jnp.dot(memory_w, v_head, preferred_element_type=jnp.float32)
            carried = jnp.zeros((count, DH), jnp.float32)
            for request_number in range(SEQS):
                adapter_term = jnp.dot(q_head, states[request_number][head], preferred_element_type=jnp.float32)
                carried = carried + member[:, request_number:request_number + 1] * adapter_term
            recalled = carried * jnp.exp(level[:, head])[:, None] + intra
            factor = lax.rsqrt(lax.optimization_barrier(jnp.mean(recalled * recalled, axis=1, keepdims=True)) + epsilon)
            outputs.append(attended + mix_gate[:, head:head + 1] * recalled * factor)
        head_out = jnp.concatenate(outputs, axis=1).astype(jnp.bfloat16)
        projected = jnp.dot(head_out, head_output_weight, preferred_element_type=jnp.float32)
        mixed = (group_rows.astype(jnp.float32) + projected).astype(jnp.bfloat16)
        normed_two = rms_scale(mixed, norm_gain_pair[1])
        gate = jnp.dot(normed_two, feedforward_weight[0], preferred_element_type=jnp.float32)
        upper = jnp.dot(normed_two, feedforward_weight[1], preferred_element_type=jnp.float32)
        hidden = (jax.nn.silu(gate) * upper).astype(jnp.bfloat16)
        feed = jnp.dot(hidden, feedforward_weight[2].T, preferred_element_type=jnp.float32)
        return (mixed.astype(jnp.float32) + feed).astype(jnp.bfloat16)
    grouped = tokens.reshape(N_REQ, TOK_GRP, MODEL_WIDTH)
    result = lax.map(group_layer, (grouped, lengths, request_adapter_index, request_cache_index))
    return result.reshape(TOKENS, MODEL_WIDTH)
```

```python
import functools
import math

import jax
import jax.numpy as jnp
from jax import lax
from jax.experimental import pallas as pl
from jax.experimental.pallas import tpu as pltpu
from jax.sharding import PartitionSpec as P

epsilon = 1e-05
MESH = pl.DeviceIdType.MESH


def rms_scale(values, gain):
    widened = values.astype(jnp.float32)
    factor = lax.rsqrt(jnp.mean(widened * widened, axis=-1, keepdims=True) + epsilon)
    return (widened * factor * gain).astype(jnp.bfloat16)


def mix_kernel(
    n, seqs, rank, heads, dh,
    lens_ref, idx_ref, tok_ref, gain_ref, aux_ref, up_ref, bias_ref, qkv_ref, cache_ref, wo_ref, ff_ref,
    out_ref, wo_other, ff_other,
    wq, auxr, upr, biasr, r1, idxb, idxs, stage, r2, q_s, k_s, v_s, att_s, intra_s,
    s1, t1, si, ti, s2, t2, sp, tp, lsem,
):
    g = lax.axis_index("req")
    c = lax.axis_index("col")
    other = 1 - c
    me = g * 2 + c
    total = n * 2
    own = cache_ref.shape[0]
    rows = tok_ref.shape[0]
    half = heads // 2
    f32, bf16 = jnp.float32, jnp.bfloat16

    barrier = pltpu.get_barrier_semaphore()

    def greet(k, carry):
        d = lax.rem(me + k, total)
        pl.semaphore_signal(barrier, inc=1, device_id=(d // 2, lax.rem(d, 2)), device_id_type=MESH)
        return carry

    local_w = pltpu.make_async_copy(qkv_ref, wq.at[c], lsem.at[0])
    local_w.start()
    local_c = pltpu.make_async_copy(cache_ref.at[:, g], r1.at[pl.ds(own * g, own)], lsem.at[1])
    local_c.start()
    local_i = pltpu.make_async_copy(idx_ref, idxb.at[g], lsem.at[2])
    local_i.start()

    lax.fori_loop(1, total, greet, 0)
    pl.semaphore_wait(barrier, total - 1)

    def cache_copy(p, slot, sem):
        return pltpu.make_async_remote_copy(
            src_ref=cache_ref.at[:, p], dst_ref=r1.at[pl.ds(own * slot, own)],
            send_sem=s1.at[p], recv_sem=t1.at[sem], device_id=(p, c), device_id_type=MESH)

    def index_copy(p, slot):
        return pltpu.make_async_remote_copy(
            src_ref=idx_ref, dst_ref=idxb.at[slot],
            send_sem=si.at[p], recv_sem=ti.at[slot], device_id=(p, c), device_id_type=MESH)

    def first(k, carry):
        p = lax.rem(g + k, n)
        index_copy(p, g).start()
        cache_copy(p, g, g).start()
        return carry

    lax.fori_loop(1, n, first, 0)

    def pair(src, dst, i):
        return pltpu.make_async_remote_copy(
            src_ref=src, dst_ref=dst, send_sem=sp.at[i], recv_sem=tp.at[i],
            device_id=(g, other), device_id_type=MESH)

    pairs = [
        pair(aux_ref.at[other], auxr, 0),
        pair(bias_ref, biasr, 1),
        pair(up_ref.at[other], upr.at[c], 2),
        pair(qkv_ref, wq.at[c], 3),
        pair(wo_ref, wo_other, 4),
        pair(ff_ref, ff_other, 5),
    ]
    for one in pairs:
        one.start()
    upr[c] = up_ref[c]

    x = tok_ref[...].astype(f32)
    factor = lax.rsqrt(jnp.mean(x * x, axis=-1, keepdims=True) + epsilon)
    normed = (x * factor * gain_ref[0:1, :]).astype(bf16)

    first_end = lens_ref[c * seqs]
    ends = [first_end]
    for j in range(1, seqs - 1):
        ends.append(ends[-1] + lens_ref[c * seqs + j])

    def segment_of(shape, axis):
        pos = lax.broadcasted_iota(jnp.int32, shape, axis)
        seg = jnp.zeros(shape, jnp.int32)
        for e in ends:
            seg = seg + (pos >= e).astype(jnp.int32)
        return pos, seg

    q_pos, q_seg = segment_of((rows, rows), 0)
    k_pos, k_seg = segment_of((rows, rows), 1)
    allowed = (q_seg == k_seg) & (k_pos <= q_pos)
    _, seg_wide = segment_of((rows, 128), 0)

    pairs[0].wait_recv()
    pairs[1].wait_recv()
    aux = aux_ref[c] + auxr[...]
    bias = bias_ref[0:1, :] + biasr[0:1, :]
    terms = jnp.dot(normed, aux, preferred_element_type=f32)
    lane = lax.broadcasted_iota(jnp.int32, (rows, 128), 1)
    mine = lane // rank == seg_wide
    low = jnp.where(mine, terms, 0.0).astype(bf16)
    shifted = terms + bias
    log_keep = jnp.minimum(shifted, 0.0) - jnp.log1p(jnp.exp(-jnp.abs(shifted)))
    mix_gate = 1.0 / (1.0 + jnp.exp(-terms))
    ones = allowed.astype(f32).astype(bf16)
    part = log_keep.astype(bf16)
    level = jnp.dot(ones, part, preferred_element_type=f32)
    rest = log_keep - part.astype(f32)
    part = rest.astype(bf16)
    level = level + jnp.dot(ones, part, preferred_element_type=f32)
    part = (rest - part.astype(f32)).astype(bf16)
    level = level + jnp.dot(ones, part, preferred_element_type=f32)
    level_t = jnp.transpose(level)
    base = seqs * rank

    pairs[2].wait_recv()
    pairs[3].wait_recv()
    local_w.wait()
    width = half * dh
    for b in range(2):
        cols = pl.ds(b * width, width)
        q = jnp.dot(normed, wq[b, 0], preferred_element_type=f32)
        q_s[:, cols] = (q + jnp.dot(low, upr[b], preferred_element_type=f32)).astype(bf16)
        k_s[:, cols] = jnp.dot(normed, wq[b, 1], preferred_element_type=f32).astype(bf16)
        v_s[:, cols] = jnp.dot(normed, wq[b, 2], preferred_element_type=f32).astype(bf16)

    local_c.wait()
    local_i.wait()

    def first_wait(k, carry):
        p = lax.rem(g + k, n)
        index_copy(p, p).wait_recv()
        cache_copy(p, p, p).wait_recv()
        return carry

    lax.fori_loop(1, n, first_wait, 0)
    to_smem = pltpu.make_async_copy(idxb, idxs, lsem.at[3])
    to_smem.start()
    to_smem.wait()

    def pick(p):
        for b in range(2):
            for j in range(seqs):
                i = idxs[p, 0, b * seqs + j]
                piece = r1[jnp.minimum(i, own * n - 1)]
                stage[p, b, j] = jnp.where(i < own * n, piece, jnp.zeros_like(piece))

    def second_copy(d, slot_c, slot_g):
        return pltpu.make_async_remote_copy(
            src_ref=stage.at[d // 2, lax.rem(d, 2)], dst_ref=r2.at[slot_c, slot_g],
            send_sem=s2.at[d], recv_sem=t2.at[slot_c * n + slot_g],
            device_id=(d // 2, lax.rem(d, 2)), device_id_type=MESH)

    def second(k, carry):
        p = lax.rem(g + k, n)
        pick(p)
        second_copy(p * 2, c, g).start()
        second_copy(p * 2 + 1, c, g).start()
        return carry

    lax.fori_loop(1, n, second, 0)
    pick(g)
    second_copy(g * 2 + other, c, g).start()
    keep = pltpu.make_async_copy(stage.at[g, c], r2.at[c, g], lsem.at[4])
    keep.start()

    scale = 1.0 / math.sqrt(dh)
    for h in range(heads):
        cols = pl.ds(h * dh, dh)
        scores = lax.dot_general(
            q_s[:, cols], k_s[:, cols], (((1,), (1,)), ((), ())), preferred_element_type=f32) * scale
        masked = jnp.where(allowed, scores, -jnp.inf)
        peak = jnp.max(masked, axis=1, keepdims=True)
        weights = jnp.exp(masked - peak)
        probs = (weights / jnp.sum(weights, axis=1, keepdims=True)).astype(bf16)
        att_s[:, cols] = jnp.dot(probs, v_s[:, cols], preferred_element_type=f32)
        gap = jnp.where(allowed, level[:, base + h:base + h + 1] - level_t[base + h:base + h + 1, :], -jnp.inf)
        memory_w = (scores * jnp.exp(gap)).astype(bf16)
        intra_s[:, cols] = jnp.dot(memory_w, v_s[:, cols], preferred_element_type=f32)

    keep.wait()

    def second_wait(k, carry):
        d = lax.rem(me + k, total)
        second_copy(d, lax.rem(d, 2), d // 2).wait_recv()
        return carry

    lax.fori_loop(1, total, second_wait, 0)

    per_head = n // half
    for h in range(heads):
        cols = pl.ds(h * dh, dh)
        q = q_s[:, cols]
        carried = jnp.zeros((rows, dh), f32)
        for j in range(seqs):
            state = r2[h // half, (h % half) * per_head:(h % half + 1) * per_head, j]
            state = state.astype(f32).reshape(dh, dh).astype(bf16)
            carried = jnp.where(seg_wide == j, jnp.dot(q, state, preferred_element_type=f32), carried)
        recalled = carried * jnp.exp(level[:, base + h:base + h + 1]) + intra_s[:, cols]
        factor = lax.rsqrt(jnp.mean(recalled * recalled, axis=1, keepdims=True) + epsilon)
        gate = mix_gate[:, base + heads + h:base + heads + h + 1]
        out_ref[:, cols] = (att_s[:, cols] + gate * recalled * factor).astype(bf16)

    def drain_first(k, carry):
        p = lax.rem(g + k, n)
        index_copy(p, g).wait_send()
        cache_copy(p, g, g).wait_send()
        return carry

    lax.fori_loop(1, n, drain_first, 0)

    def drain_second(k, carry):
        second_copy(lax.rem(me + k, total), c, g).wait_send()
        return carry

    lax.fori_loop(1, total, drain_second, 0)
    for one in pairs:
        one.wait_send()
    pairs[4].wait_recv()
    pairs[5].wait_recv()


def on_device(
    tokens, norm_gain_pair, query_key_value_weight, head_gate_weight, decay_logit_bias,
    adapter_down_factor, adapter_up_factor, lengths, request_adapter_index, request_cache_index,
    caches, head_output_weight, feedforward_weight,
):
    n = lax.axis_size("req")
    c = lax.axis_index("col")
    rows, width = tokens.shape
    seqs = lengths.shape[2]
    adapters, _, rank = adapter_down_factor.shape
    local_heads = head_gate_weight.shape[2]
    heads = 2 * local_heads
    head_cols = query_key_value_weight.shape[2]
    dh = head_cols // local_heads
    own = caches.shape[0]
    piece = local_heads * dh // n
    bf16 = jnp.bfloat16

    which = request_adapter_index[0]
    local = which - c * adapters
    held = (local >= 0) & (local < adapters)
    picked = [
        jnp.where(held[s], lax.dynamic_index_in_dim(
            adapter_down_factor, jnp.clip(local[s], 0, adapters - 1), 0, keepdims=False), 0).astype(bf16)
        for s in range(2 * seqs)
    ]
    used = seqs * rank
    gates = jnp.zeros((2, width, 2, local_heads), bf16)
    gates = jnp.where(jnp.arange(2)[None, None, :, None] == c, head_gate_weight[:, :, None, :], gates)
    gates = gates.reshape(2, width, heads)
    filler = jnp.zeros((width, 128 - used - 2 * heads), bf16)
    aux = jnp.stack([
        jnp.concatenate(picked[b * seqs:(b + 1) * seqs] + [gates[0], gates[1], filler], axis=1) for b in range(2)])
    up = [lax.dynamic_index_in_dim(adapter_up_factor, which[s], 0, keepdims=False) for s in range(2 * seqs)]
    blank = jnp.zeros((128 - used, head_cols), bf16)
    up = jnp.stack([jnp.concatenate(up[b * seqs:(b + 1) * seqs] + [blank], axis=0) for b in range(2)])
    bias = jnp.where(jnp.arange(2)[:, None] == c, decay_logit_bias[None, :], 0.0).reshape(heads)
    bias = jnp.broadcast_to(jnp.pad(bias, (used, 128 - used - heads))[None], (8, 128))
    index = jnp.broadcast_to(jnp.pad(request_cache_index[0], (0, 128 - 2 * seqs))[None], (8, 128))

    vmem = pl.BlockSpec(memory_space=pltpu.VMEM)
    smem = pl.BlockSpec(memory_space=pltpu.SMEM)
    hbm = pl.BlockSpec(memory_space=pl.ANY)
    dma = pltpu.SemaphoreType.DMA
    head_out, wo_other, ff_other = pl.pallas_call(
        functools.partial(mix_kernel, n, seqs, rank, heads, dh),
        out_shape=(
            jax.ShapeDtypeStruct((rows, heads * dh), bf16),
            jax.ShapeDtypeStruct(head_output_weight.shape, bf16),
            jax.ShapeDtypeStruct(feedforward_weight.shape, bf16),
        ),
        in_specs=[smem, vmem, vmem, vmem, vmem, vmem, vmem, hbm, hbm, hbm, hbm],
        out_specs=(vmem, hbm, hbm),
        scratch_shapes=[
            pltpu.VMEM((2,) + query_key_value_weight.shape, bf16),
            pltpu.VMEM((width, 128), bf16),
            pltpu.VMEM((2, 128, head_cols), bf16),
            pltpu.VMEM((8, 128), jnp.float32),
            pltpu.VMEM((own * n, piece, dh), bf16),
            pltpu.VMEM((n, 8, 128), jnp.int32),
            pltpu.SMEM((n, 8, 128), jnp.int32),
            pltpu.VMEM((n, 2, seqs, piece, dh), bf16),
            pltpu.VMEM((2, n, seqs, piece, dh), bf16),
            pltpu.VMEM((rows, heads * dh), bf16),
            pltpu.VMEM((rows, heads * dh), bf16),
            pltpu.VMEM((rows, heads * dh), bf16),
            pltpu.VMEM((rows, heads * dh), jnp.float32),
            pltpu.VMEM((rows, heads * dh), jnp.float32),
            dma((n,)), dma((n,)), dma((n,)), dma((n,)), dma((2 * n,)), dma((2 * n,)), dma((6,)), dma((6,)), dma((5,)),
        ],
        compiler_params=pltpu.CompilerParams(
            collective_id=0, has_side_effects=True, vmem_limit_bytes=50 * 2**20),
        cost_estimate=pl.CostEstimate(flops=2 * 10**9, bytes_accessed=2 * 10**7, transcendentals=10**6),
    )(
        lengths.reshape(-1), index, tokens, norm_gain_pair, aux, up, bias, query_key_value_weight,
        caches.reshape(own, n, piece, dh), head_output_weight, feedforward_weight,
    )

    def by_owner(mine, theirs, axis):
        return (jnp.where(c == 0, mine, theirs), jnp.where(c == 0, theirs, mine))

    left, right = head_out[:, :head_cols], head_out[:, head_cols:]
    near, far = by_owner(left, right, 1)
    f32 = jnp.float32
    proj = jnp.dot(near, head_output_weight, preferred_element_type=f32) + jnp.dot(
        far, wo_other, preferred_element_type=f32)
    mixed = (tokens.astype(f32) + proj).astype(bf16)
    normed_two = rms_scale(mixed, norm_gain_pair[1])
    feed = mixed.astype(f32)
    for weight in (feedforward_weight, ff_other):
        gate_up = jnp.einsum("td,kdf->ktf", normed_two, weight[:2], preferred_element_type=f32)
        hidden = (jax.nn.silu(gate_up[0]) * gate_up[1]).astype(bf16)
        feed = feed + jnp.einsum("tf,df->td", hidden, weight[2], preferred_element_type=f32)
    return feed.astype(bf16)


def solution(mesh):
    placed = (
        P(("req", "col"), None),
        P(),
        P(None, None, "col"),
        P(None, None, "col"),
        P("col"),
        P("col", None, None),
        P(None, None, "col"),
        P("req", None, None),
        P("req", None),
        P("req", None),
        P("req", "col", None, None),
        P("col", None),
        P(None, None, "col"),
    )
    return jax.shard_map(
        on_device, mesh=mesh, in_specs=placed, out_specs=P(("req", "col"), None), check_vma=False
    )
```

```python
import functools
import math

import jax
import jax.numpy as jnp
from jax import lax
from jax.experimental import pallas as pl
from jax.experimental.pallas import tpu as pltpu
from jax.sharding import PartitionSpec as P

epsilon = 1e-05
MESH = pl.DeviceIdType.MESH


def mix_kernel(
    n, seqs, rank, half, dh,
    lens_ref, aidx_ref, cidx_ref, bias_ref, tok_ref, gain_ref, gate_ref, down_ref, up_ref,
    qkv_ref, cache_ref, wo_ref, ff_ref,
    out_ref,
    down_v, up_v, aux_s, auxr, upsel, upr, biasr, gates, wq, wo, wff, r1, idxb, idxs, stage, r2,
    q_s, k_s, v_s, att_s, intra_s, head_s,
    s1, t1, si, ti, s2, t2, sp, tp, lsem,
):
    g = lax.axis_index("req")
    c = lax.axis_index("col")
    other = 1 - c
    me = g * 2 + c
    total = n * 2
    own = cache_ref.shape[0]
    rows = tok_ref.shape[0]
    adapters = down_ref.shape[0]
    base = seqs * rank
    f32, bf16 = jnp.float32, jnp.bfloat16

    barrier = pltpu.get_barrier_semaphore()

    def greet(k, carry):
        d = lax.rem(me + k, total)
        pl.semaphore_signal(barrier, inc=1, device_id=(d // 2, lax.rem(d, 2)), device_id_type=MESH)
        return carry

    lax.fori_loop(1, total, greet, 0)

    def local(src, dst, i):
        one = pltpu.make_async_copy(src, dst, lsem.at[i])
        one.start()
        return one

    local_down = local(down_ref, down_v, 0)
    local_up = local(up_ref, up_v, 1)
    local_c = local(cache_ref.at[:, g], r1.at[pl.ds(own * g, own)], 2)
    local_w = local(qkv_ref, wq.at[0], 3)
    local_wo = local(wo_ref, wo.at[0], 4)
    local_ff = local(ff_ref, wff.at[0], 5)

    lane8 = lax.broadcasted_iota(jnp.int32, (8, 128), 1)
    index = jnp.zeros((8, 128), jnp.int32)
    for s in range(2 * seqs):
        index = jnp.where(lane8 == s, cidx_ref[0, s], index)
    idxb[g] = index
    bias = jnp.zeros((8, 128), f32)
    for h in range(half):
        bias = jnp.where(lane8 == h, bias_ref[h], bias)
    biasr[0] = bias
    gates[0] = gate_ref[...]

    pl.semaphore_wait(barrier, total - 1)

    def cache_copy(p, slot):
        return pltpu.make_async_remote_copy(
            src_ref=cache_ref.at[:, p], dst_ref=r1.at[pl.ds(own * slot, own)],
            send_sem=s1.at[p], recv_sem=t1.at[slot], device_id=(p, c), device_id_type=MESH)

    def index_copy(p, slot):
        return pltpu.make_async_remote_copy(
            src_ref=idxb.at[g], dst_ref=idxb.at[slot],
            send_sem=si.at[p], recv_sem=ti.at[slot], device_id=(p, c), device_id_type=MESH)

    def first(k, carry):
        p = lax.rem(g + k, n)
        index_copy(p, g).start()
        cache_copy(p, g).start()
        return carry

    lax.fori_loop(1, n, first, 0)

    pairs = []

    def pair(src, dst):
        i = len(pairs)
        one = pltpu.make_async_remote_copy(
            src_ref=src, dst_ref=dst, send_sem=sp.at[i], recv_sem=tp.at[i],
            device_id=(g, other), device_id_type=MESH)
        one.start()
        pairs.append(one)
        return one

    pair_gates = pair(gates.at[0], gates.at[1])
    pair_bias = pair(biasr.at[0], biasr.at[1])

    local_down.wait()
    local_up.wait()
    for b in range(2):
        for j in range(seqs):
            a = aidx_ref[0, b * seqs + j]
            mine_at = a - c * adapters
            held = (mine_at >= 0) & (mine_at < adapters)
            factor = down_v[jnp.clip(mine_at, 0, adapters - 1)]
            aux_s[b, j * rank:(j + 1) * rank, :] = jnp.where(held, factor, jnp.zeros_like(factor))
            upsel[b, j * rank:(j + 1) * rank, :] = up_v[a]
    pair_aux = pair(aux_s.at[other], auxr)
    pair_up = pair(upsel.at[other], upr)
    pair_w = pair(qkv_ref, wq.at[1])
    pair_wo = pair(wo_ref, wo.at[1])
    pair_ff = [pair(ff_ref.at[k], wff.at[1, k]) for k in range(3)]

    x = tok_ref[...].astype(f32)
    factor = lax.rsqrt(jnp.mean(x * x, axis=-1, keepdims=True) + epsilon)
    normed = (x * factor * gain_ref[0:1, :]).astype(bf16)

    ends = [lens_ref[0, c, 0]]
    for j in range(1, seqs - 1):
        ends.append(ends[-1] + lens_ref[0, c, j])

    def segment_of(shape, axis):
        pos = lax.broadcasted_iota(jnp.int32, shape, axis)
        seg = jnp.zeros(shape, jnp.int32)
        for e in ends:
            seg = seg + (pos >= e).astype(jnp.int32)
        return pos, seg

    q_pos, q_seg = segment_of((rows, rows), 0)
    k_pos, k_seg = segment_of((rows, rows), 1)
    allowed = (q_seg == k_seg) & (k_pos <= q_pos)
    _, seg_wide = segment_of((rows, 128), 0)
    _, seg_low = segment_of((rows, base), 0)

    local_w.wait()
    width = half * dh
    cols = pl.ds(0, width)
    own_q = jnp.dot(normed, wq[0, 0], preferred_element_type=f32)
    k_s[:, cols] = jnp.dot(normed, wq[0, 1], preferred_element_type=f32).astype(bf16)
    v_s[:, cols] = jnp.dot(normed, wq[0, 2], preferred_element_type=f32).astype(bf16)

    pair_gates.wait_recv()
    pair_bias.wait_recv()
    pair_aux.wait_recv()
    pair_up.wait_recv()
    nt = (((1,), (1,)), ((), ()))
    down = aux_s[c] + auxr[...]
    low = lax.dot_general(normed, down, nt, preferred_element_type=f32)
    lane = lax.broadcasted_iota(jnp.int32, (rows, base), 1)
    low = jnp.where(lane // rank == seg_low, low, 0.0).astype(bf16)
    own_q = own_q + jnp.dot(low, upsel[c], preferred_element_type=f32)
    q_s[:, cols] = own_q.astype(bf16)

    ones = allowed.astype(f32).astype(bf16)
    levels, levels_t, mixes = [], [], []
    for b in range(2):
        terms = lax.dot_general(normed, gates[b], nt, preferred_element_type=f32)
        shifted = terms + biasr[b][0:1, :]
        log_keep = jnp.minimum(shifted, 0.0) - jnp.log1p(jnp.exp(-jnp.abs(shifted)))
        mixes.append(1.0 / (1.0 + jnp.exp(-terms)))
        part = log_keep.astype(bf16)
        level = jnp.dot(ones, part, preferred_element_type=f32)
        rest = log_keep - part.astype(f32)
        part = rest.astype(bf16)
        level = level + jnp.dot(ones, part, preferred_element_type=f32)
        part = (rest - part.astype(f32)).astype(bf16)
        level = level + jnp.dot(ones, part, preferred_element_type=f32)
        levels.append(level)
        levels_t.append(jnp.transpose(level))

    local_c.wait()

    def first_wait(k, carry):
        p = lax.rem(g + k, n)
        index_copy(p, p).wait_recv()
        cache_copy(p, p).wait_recv()
        return carry

    lax.fori_loop(1, n, first_wait, 0)
    local(idxb, idxs, 6).wait()

    def pick(p):
        for b in range(2):
            for j in range(seqs):
                i = idxs[p, 0, b * seqs + j]
                piece = r1[jnp.minimum(i, own * n - 1)]
                stage[p, b, j] = jnp.where(i < own * n, piece, jnp.zeros_like(piece))

    def second_copy(d, slot_c, slot_g):
        return pltpu.make_async_remote_copy(
            src_ref=stage.at[d // 2, lax.rem(d, 2)], dst_ref=r2.at[slot_c, slot_g],
            send_sem=s2.at[d], recv_sem=t2.at[slot_c * n + slot_g],
            device_id=(d // 2, lax.rem(d, 2)), device_id_type=MESH)

    def second(k, carry):
        p = lax.rem(g + k, n)
        pick(p)
        second_copy(p * 2 + c, 0, g).start()
        second_copy(p * 2 + other, 1, g).start()
        return carry

    lax.fori_loop(1, n, second, 0)
    pick(g)
    second_copy(g * 2 + other, 1, g).start()
    keep = local(stage.at[g, c], r2.at[0, g], 7)

    scale = 1.0 / math.sqrt(dh)

    def attend(h):
        cols = pl.ds(h * dh, dh)
        b, i = h // half, h % half
        scores = lax.dot_general(q_s[:, cols], k_s[:, cols], nt, preferred_element_type=f32) * scale
        masked = jnp.where(allowed, scores, -jnp.inf)
        peak = jnp.max(masked, axis=1, keepdims=True)
        weights = jnp.exp(masked - peak)
        probs = (weights / jnp.sum(weights, axis=1, keepdims=True)).astype(bf16)
        att_s[:, cols] = jnp.dot(probs, v_s[:, cols], preferred_element_type=f32)
        gap = jnp.where(allowed, levels[b][:, i:i + 1] - levels_t[b][i:i + 1, :], -jnp.inf)
        memory_w = (scores * jnp.exp(gap)).astype(bf16)
        intra_s[:, cols] = jnp.dot(memory_w, v_s[:, cols], preferred_element_type=f32)

    for h in range(half):
        attend(h)
    pair_w.wait_recv()
    cols = pl.ds(width, width)
    q = jnp.dot(normed, wq[1, 0], preferred_element_type=f32)
    q_s[:, cols] = (q + jnp.dot(low, upr[...], preferred_element_type=f32)).astype(bf16)
    k_s[:, cols] = jnp.dot(normed, wq[1, 1], preferred_element_type=f32).astype(bf16)
    v_s[:, cols] = jnp.dot(normed, wq[1, 2], preferred_element_type=f32).astype(bf16)
    for h in range(half, 2 * half):
        attend(h)

    keep.wait()

    def second_wait(k, carry):
        p = lax.rem(g + k, n)
        second_copy(p * 2 + c, 0, p).wait_recv()
        second_copy(p * 2 + other, 1, p).wait_recv()
        return carry

    lax.fori_loop(1, n, second_wait, 0)
    second_copy(g * 2 + other, 1, g).wait_recv()

    per_head = n // half
    for h in range(2 * half):
        cols = pl.ds(h * dh, dh)
        b, i = h // half, h % half
        q = q_s[:, cols]
        carried = jnp.zeros((rows, dh), f32)
        for j in range(seqs):
            state = r2[b, i * per_head:(i + 1) * per_head, j]
            state = state.astype(f32).reshape(dh, dh).astype(bf16)
            carried = jnp.where(seg_wide == j, jnp.dot(q, state, preferred_element_type=f32), carried)
        recalled = carried * jnp.exp(levels[b][:, i:i + 1]) + intra_s[:, cols]
        factor = lax.rsqrt(jnp.mean(recalled * recalled, axis=1, keepdims=True) + epsilon)
        head_s[:, cols] = (att_s[:, cols] + mixes[b][:, half + i:half + i + 1] * recalled * factor).astype(bf16)

    local_wo.wait()
    pair_wo.wait_recv()
    proj = jnp.dot(head_s[:, :width], wo[0], preferred_element_type=f32)
    proj = proj + jnp.dot(head_s[:, width:], wo[1], preferred_element_type=f32)
    mixed = (tok_ref[...].astype(f32) + proj).astype(bf16).astype(f32)
    factor = lax.rsqrt(jnp.mean(mixed * mixed, axis=-1, keepdims=True) + epsilon)
    normed_two = (mixed * factor * gain_ref[1:2, :]).astype(bf16)
    feed = mixed
    local_ff.wait()
    for b in range(2):
        if b == 1:
            pair_ff[0].wait_recv()
        gate = jnp.dot(normed_two, wff[b, 0], preferred_element_type=f32)
        if b == 1:
            pair_ff[1].wait_recv()
        upper = jnp.dot(normed_two, wff[b, 1], preferred_element_type=f32)
        hidden = (gate / (1.0 + jnp.exp(-gate)) * upper).astype(bf16)
        if b == 1:
            pair_ff[2].wait_recv()
        feed = feed + lax.dot_general(hidden, wff[b, 2], nt, preferred_element_type=f32)
    out_ref[...] = feed.astype(bf16)

    def drain(k, carry):
        p = lax.rem(g + k, n)
        index_copy(p, g).wait_send()
        cache_copy(p, g).wait_send()
        second_copy(p * 2 + c, 0, g).wait_send()
        second_copy(p * 2 + other, 1, g).wait_send()
        return carry

    lax.fori_loop(1, n, drain, 0)
    second_copy(g * 2 + other, 1, g).wait_send()
    for one in pairs:
        one.wait_send()


def on_device(
    tokens, norm_gain_pair, query_key_value_weight, head_gate_weight, decay_logit_bias,
    adapter_down_factor, adapter_up_factor, lengths, request_adapter_index, request_cache_index,
    caches, head_output_weight, feedforward_weight,
):
    n = lax.axis_size("req")
    rows, width = tokens.shape
    seqs = lengths.shape[2]
    adapters, _, rank = adapter_down_factor.shape
    half = head_gate_weight.shape[2]
    head_cols = query_key_value_weight.shape[2]
    dh = head_cols // half
    own = caches.shape[0]
    piece = half * dh // n
    base = seqs * rank
    bf16, f32 = jnp.bfloat16, jnp.float32

    gate = head_gate_weight.transpose(0, 2, 1).reshape(2 * half, width)
    gate = jnp.pad(gate, ((0, 128 - 2 * half), (0, 0)))

    vmem = pl.BlockSpec(memory_space=pltpu.VMEM)
    smem = pl.BlockSpec(memory_space=pltpu.SMEM)
    hbm = pl.BlockSpec(memory_space=pl.ANY)
    dma = pltpu.SemaphoreType.DMA
    wide = 2 * head_cols
    return pl.pallas_call(
        functools.partial(mix_kernel, n, seqs, rank, half, dh),
        out_shape=jax.ShapeDtypeStruct((rows, width), bf16),
        in_specs=[smem] * 4 + [vmem] * 3 + [hbm] * 6,
        out_specs=vmem,
        scratch_shapes=[
            pltpu.VMEM((adapters, rank, width), bf16),
            pltpu.VMEM(adapter_up_factor.shape, bf16),
            pltpu.VMEM((2, base, width), bf16),
            pltpu.VMEM((base, width), bf16),
            pltpu.VMEM((2, base, head_cols), bf16),
            pltpu.VMEM((base, head_cols), bf16),
            pltpu.VMEM((2, 8, 128), f32),
            pltpu.VMEM((2, 128, width), bf16),
            pltpu.VMEM((2,) + query_key_value_weight.shape, bf16),
            pltpu.VMEM((2,) + head_output_weight.shape, bf16),
            pltpu.VMEM((2,) + feedforward_weight.shape, bf16),
            pltpu.VMEM((own * n, piece, dh), bf16),
            pltpu.VMEM((n, 8, 128), jnp.int32),
            pltpu.SMEM((n, 8, 128), jnp.int32),
            pltpu.VMEM((n, 2, seqs, piece, dh), bf16),
            pltpu.VMEM((2, n, seqs, piece, dh), bf16),
            pltpu.VMEM((rows, wide), bf16),
            pltpu.VMEM((rows, wide), bf16),
            pltpu.VMEM((rows, wide), bf16),
            pltpu.VMEM((rows, wide), f32),
            pltpu.VMEM((rows, wide), f32),
            pltpu.VMEM((rows, wide), bf16),
            dma((n,)), dma((n,)), dma((n,)), dma((n,)), dma((2 * n,)), dma((2 * n,)),
            dma((10,)), dma((10,)), dma((8,)),
        ],
        compiler_params=pltpu.CompilerParams(
            collective_id=0, has_side_effects=True, vmem_limit_bytes=56 * 2**20),
        cost_estimate=pl.CostEstimate(flops=7 * 10**9, bytes_accessed=3 * 10**7, transcendentals=10**6),
    )(
        lengths, request_adapter_index, request_cache_index, decay_logit_bias, tokens, norm_gain_pair,
        gate, adapter_down_factor.transpose(0, 2, 1), adapter_up_factor, query_key_value_weight,
        caches.reshape(own, n, piece, dh), head_output_weight, feedforward_weight,
    )


def solution(mesh):
    placed = (
        P(("req", "col"), None),
        P(),
        P(None, None, "col"),
        P(None, None, "col"),
        P("col"),
        P("col", None, None),
        P(None, None, "col"),
        P("req", None, None),
        P("req", None),
        P("req", None),
        P("req", "col", None, None),
        P("col", None),
        P(None, None, "col"),
    )
    return jax.shard_map(
        on_device, mesh=mesh, in_specs=placed, out_specs=P(("req", "col"), None), check_vma=False
    )
```

```python
import functools
import math

import jax
import jax.numpy as jnp
from jax import lax
from jax.experimental import pallas as pl
from jax.experimental.pallas import tpu as pltpu
from jax.sharding import PartitionSpec as P

epsilon = 1e-05
MESH = pl.DeviceIdType.MESH


def mix_kernel(
    n, seqs, rank, half, dh,
    lens_ref, aidx_ref, cidx_ref, bias_ref, tok_ref, gain_ref, gate_ref, down_ref, up_ref,
    qkv_ref, cache_ref, wo_ref, ff_ref,
    out_ref,
    down_v, up_v, aux_s, auxr, upsel, upr, biasr, gates, wq, wo, wff, r1, idxb, idxs, stage, r2,
    q_s, k_s, v_s, att_s, intra_s, head_s,
    s1, t1, si, ti, s2, t2, sp, tp, lsem,
):
    g = lax.axis_index("req")
    c = lax.axis_index("col")
    other = 1 - c
    me = g * 2 + c
    total = n * 2
    own = cache_ref.shape[0]
    rows = tok_ref.shape[0]
    adapters = down_ref.shape[0]
    base = seqs * rank
    f32, bf16 = jnp.float32, jnp.bfloat16

    barrier = pltpu.get_barrier_semaphore()

    def greet(k, carry):
        d = lax.rem(me + k, total)
        pl.semaphore_signal(barrier, inc=1, device_id=(d // 2, lax.rem(d, 2)), device_id_type=MESH)
        return carry

    lax.fori_loop(1, total, greet, 0)

    def local(src, dst, i):
        one = pltpu.make_async_copy(src, dst, lsem.at[i])
        one.start()
        return one

    local_down = local(down_ref, down_v, 0)
    local_up = local(up_ref, up_v, 1)
    local_c = local(cache_ref.at[:, g], r1.at[pl.ds(own * g, own)], 2)
    local_w = local(qkv_ref, wq.at[0], 3)
    local_wo = local(wo_ref, wo.at[0], 4)
    local_ff = local(ff_ref, wff.at[0], 5)

    lane8 = lax.broadcasted_iota(jnp.int32, (8, 128), 1)
    index = jnp.zeros((8, 128), jnp.int32)
    for s in range(2 * seqs):
        index = jnp.where(lane8 == s, cidx_ref[0, s], index)
    idxb[g] = index
    bias = jnp.zeros((8, 128), f32)
    for h in range(half):
        bias = jnp.where(lane8 == h, bias_ref[h], bias)
    biasr[0] = bias
    zeros = jnp.zeros((128 - 2 * half, gate_ref.shape[2]), f32)
    gates[0] = jnp.concatenate([gate_ref[0].astype(f32), gate_ref[1].astype(f32), zeros], axis=0).astype(bf16)

    pl.semaphore_wait(barrier, total - 1)

    def cache_copy(p, slot):
        return pltpu.make_async_remote_copy(
            src_ref=cache_ref.at[:, p], dst_ref=r1.at[pl.ds(own * slot, own)],
            send_sem=s1.at[p], recv_sem=t1.at[slot], device_id=(p, c), device_id_type=MESH)

    def index_copy(p, slot):
        return pltpu.make_async_remote_copy(
            src_ref=idxb.at[g], dst_ref=idxb.at[slot],
            send_sem=si.at[p], recv_sem=ti.at[slot], device_id=(p, c), device_id_type=MESH)

    def first(k, carry):
        p = lax.rem(g + k, n)
        index_copy(p, g).start()
        cache_copy(p, g).start()
        return carry

    lax.fori_loop(1, n, first, 0)

    pairs = []

    def pair(src, dst):
        i = len(pairs)
        one = pltpu.make_async_remote_copy(
            src_ref=src, dst_ref=dst, send_sem=sp.at[i], recv_sem=tp.at[i],
            device_id=(g, other), device_id_type=MESH)
        one.start()
        pairs.append(one)
        return one

    pair_gates = pair(gates.at[0], gates.at[1])
    pair_bias = pair(biasr.at[0], biasr.at[1])

    local_down.wait()
    local_up.wait()
    for b in range(2):
        for j in range(seqs):
            a = aidx_ref[0, b * seqs + j]
            mine_at = a - c * adapters
            held = (mine_at >= 0) & (mine_at < adapters)
            factor = down_v[jnp.clip(mine_at, 0, adapters - 1)]
            aux_s[b, j * rank:(j + 1) * rank, :] = jnp.where(held, factor, jnp.zeros_like(factor))
            upsel[b, j * rank:(j + 1) * rank, :] = up_v[a]
    pair_aux = pair(aux_s.at[other], auxr)
    pair_up = pair(upsel.at[other], upr)
    pair_w = pair(qkv_ref, wq.at[1])
    pair_wo = pair(wo_ref, wo.at[1])
    pair_ff = [pair(ff_ref.at[0], wff.at[1, 0])]

    x = tok_ref[...].astype(f32)
    factor = lax.rsqrt(jnp.mean(x * x, axis=-1, keepdims=True) + epsilon)
    normed = (x * factor * gain_ref[0:1, :]).astype(bf16)

    ends = [lens_ref[0, c, 0]]
    for j in range(1, seqs - 1):
        ends.append(ends[-1] + lens_ref[0, c, j])

    def segment_of(shape, axis):
        pos = lax.broadcasted_iota(jnp.int32, shape, axis)
        seg = jnp.zeros(shape, jnp.int32)
        for e in ends:
            seg = seg + (pos >= e).astype(jnp.int32)
        return pos, seg

    q_pos, q_seg = segment_of((rows, rows), 0)
    k_pos, k_seg = segment_of((rows, rows), 1)
    allowed = (q_seg == k_seg) & (k_pos <= q_pos)
    _, seg_wide = segment_of((rows, 128), 0)
    _, seg_low = segment_of((rows, base), 0)

    local_w.wait()
    width = half * dh
    cols = pl.ds(0, width)
    own_q = jnp.dot(normed, wq[0, 0], preferred_element_type=f32)
    k_s[:, cols] = jnp.dot(normed, wq[0, 1], preferred_element_type=f32).astype(bf16)
    v_s[:, cols] = jnp.dot(normed, wq[0, 2], preferred_element_type=f32).astype(bf16)

    pair_gates.wait_recv()
    pair_bias.wait_recv()
    pair_aux.wait_recv()
    pair_up.wait_recv()
    nt = (((1,), (1,)), ((), ()))
    down = aux_s[c] + auxr[...]
    low = lax.dot_general(normed, down, nt, preferred_element_type=f32)
    lane = lax.broadcasted_iota(jnp.int32, (rows, base), 1)
    low = jnp.where(lane // rank == seg_low, low, 0.0).astype(bf16)
    own_q = own_q + jnp.dot(low, upsel[c], preferred_element_type=f32)
    q_s[:, cols] = own_q.astype(bf16)

    ones = allowed.astype(f32).astype(bf16)
    levels, levels_t, mixes = [], [], []
    for b in range(2):
        terms = lax.dot_general(normed, gates[b], nt, preferred_element_type=f32)
        shifted = terms + biasr[b][0:1, :]
        log_keep = jnp.minimum(shifted, 0.0) - jnp.log1p(jnp.exp(-jnp.abs(shifted)))
        mixes.append(1.0 / (1.0 + jnp.exp(-terms)))
        part = log_keep.astype(bf16)
        level = jnp.dot(ones, part, preferred_element_type=f32)
        rest = log_keep - part.astype(f32)
        part = rest.astype(bf16)
        level = level + jnp.dot(ones, part, preferred_element_type=f32)
        part = (rest - part.astype(f32)).astype(bf16)
        level = level + jnp.dot(ones, part, preferred_element_type=f32)
        levels.append(level)
        levels_t.append(jnp.transpose(level))

    local_c.wait()

    def first_wait(k, carry):
        p = lax.rem(g + k, n)
        index_copy(p, p).wait_recv()
        cache_copy(p, p).wait_recv()
        return carry

    lax.fori_loop(1, n, first_wait, 0)
    local(idxb, idxs, 6).wait()

    def pick(p):
        for b in range(2):
            for j in range(seqs):
                i = idxs[p, 0, b * seqs + j]
                piece = r1[jnp.minimum(i, own * n - 1)]
                stage[p, b, j] = jnp.where(i < own * n, piece, jnp.zeros_like(piece))

    def second_copy(d, slot_c, slot_g):
        return pltpu.make_async_remote_copy(
            src_ref=stage.at[d // 2, lax.rem(d, 2)], dst_ref=r2.at[slot_c, slot_g],
            send_sem=s2.at[d], recv_sem=t2.at[slot_c * n + slot_g],
            device_id=(d // 2, lax.rem(d, 2)), device_id_type=MESH)

    def second(k, carry):
        p = lax.rem(g + k, n)
        pick(p)
        second_copy(p * 2 + c, 0, g).start()
        second_copy(p * 2 + other, 1, g).start()
        return carry

    lax.fori_loop(1, n, second, 0)
    pick(g)
    second_copy(g * 2 + other, 1, g).start()
    keep = local(stage.at[g, c], r2.at[0, g], 7)
    pair_ff += [pair(ff_ref.at[k], wff.at[1, k]) for k in range(1, 3)]

    scale = 1.0 / math.sqrt(dh)

    def attend(h):
        cols = pl.ds(h * dh, dh)
        b, i = h // half, h % half
        scores = lax.dot_general(q_s[:, cols], k_s[:, cols], nt, preferred_element_type=f32) * scale
        masked = jnp.where(allowed, scores, -jnp.inf)
        peak = jnp.max(masked, axis=1, keepdims=True)
        weights = jnp.exp(masked - peak)
        probs = (weights / jnp.sum(weights, axis=1, keepdims=True)).astype(bf16)
        att_s[:, cols] = jnp.dot(probs, v_s[:, cols], preferred_element_type=f32)
        gap = jnp.where(allowed, levels[b][:, i:i + 1] - levels_t[b][i:i + 1, :], -jnp.inf)
        memory_w = (scores * jnp.exp(gap)).astype(bf16)
        intra_s[:, cols] = jnp.dot(memory_w, v_s[:, cols], preferred_element_type=f32)

    for h in range(half):
        attend(h)
    pair_w.wait_recv()
    cols = pl.ds(width, width)
    q = jnp.dot(normed, wq[1, 0], preferred_element_type=f32)
    q_s[:, cols] = (q + jnp.dot(low, upr[...], preferred_element_type=f32)).astype(bf16)
    k_s[:, cols] = jnp.dot(normed, wq[1, 1], preferred_element_type=f32).astype(bf16)
    v_s[:, cols] = jnp.dot(normed, wq[1, 2], preferred_element_type=f32).astype(bf16)
    for h in range(half, 2 * half):
        attend(h)

    keep.wait()

    def second_wait(k, carry):
        p = lax.rem(g + k, n)
        second_copy(p * 2 + c, 0, p).wait_recv()
        second_copy(p * 2 + other, 1, p).wait_recv()
        return carry

    lax.fori_loop(1, n, second_wait, 0)
    second_copy(g * 2 + other, 1, g).wait_recv()

    per_head = n // half
    for h in range(2 * half):
        cols = pl.ds(h * dh, dh)
        b, i = h // half, h % half
        q = q_s[:, cols]
        carried = jnp.zeros((rows, dh), f32)
        for j in range(seqs):
            state = r2[b, i * per_head:(i + 1) * per_head, j]
            state = state.astype(f32).reshape(dh, dh).astype(bf16)
            carried = jnp.where(seg_wide == j, jnp.dot(q, state, preferred_element_type=f32), carried)
        recalled = carried * jnp.exp(levels[b][:, i:i + 1]) + intra_s[:, cols]
        factor = lax.rsqrt(jnp.mean(recalled * recalled, axis=1, keepdims=True) + epsilon)
        head_s[:, cols] = (att_s[:, cols] + mixes[b][:, half + i:half + i + 1] * recalled * factor).astype(bf16)

    local_wo.wait()
    pair_wo.wait_recv()
    proj = jnp.dot(head_s[:, :width], wo[0], preferred_element_type=f32)
    proj = proj + jnp.dot(head_s[:, width:], wo[1], preferred_element_type=f32)
    mixed = (tok_ref[...].astype(f32) + proj).astype(bf16).astype(f32)
    factor = lax.rsqrt(jnp.mean(mixed * mixed, axis=-1, keepdims=True) + epsilon)
    normed_two = (mixed * factor * gain_ref[1:2, :]).astype(bf16)
    feed = mixed
    local_ff.wait()
    for b in range(2):
        if b == 1:
            pair_ff[0].wait_recv()
        gate = jnp.dot(normed_two, wff[b, 0], preferred_element_type=f32)
        if b == 1:
            pair_ff[1].wait_recv()
        upper = jnp.dot(normed_two, wff[b, 1], preferred_element_type=f32)
        hidden = (gate / (1.0 + jnp.exp(-gate)) * upper).astype(bf16)
        if b == 1:
            pair_ff[2].wait_recv()
        feed = feed + lax.dot_general(hidden, wff[b, 2], nt, preferred_element_type=f32)
    out_ref[...] = feed

    def drain(k, carry):
        p = lax.rem(g + k, n)
        index_copy(p, g).wait_send()
        cache_copy(p, g).wait_send()
        second_copy(p * 2 + c, 0, g).wait_send()
        second_copy(p * 2 + other, 1, g).wait_send()
        return carry

    lax.fori_loop(1, n, drain, 0)
    second_copy(g * 2 + other, 1, g).wait_send()
    for one in pairs:
        one.wait_send()


def on_device(
    tokens, norm_gain_pair, query_key_value_weight, head_gate_weight, decay_logit_bias,
    adapter_down_factor, adapter_up_factor, lengths, request_adapter_index, request_cache_index,
    caches, head_output_weight, feedforward_weight,
):
    n = lax.axis_size("req")
    rows, width = tokens.shape
    seqs = lengths.shape[2]
    adapters, _, rank = adapter_down_factor.shape
    half = head_gate_weight.shape[2]
    head_cols = query_key_value_weight.shape[2]
    dh = head_cols // half
    own = caches.shape[0]
    piece = half * dh // n
    base = seqs * rank
    bf16, f32 = jnp.bfloat16, jnp.float32

    vmem = pl.BlockSpec(memory_space=pltpu.VMEM)
    smem = pl.BlockSpec(memory_space=pltpu.SMEM)
    hbm = pl.BlockSpec(memory_space=pl.ANY)
    dma = pltpu.SemaphoreType.DMA
    wide = 2 * head_cols
    layer = pl.pallas_call(
        functools.partial(mix_kernel, n, seqs, rank, half, dh),
        out_shape=jax.ShapeDtypeStruct((rows, width), f32),
        in_specs=[smem] * 4 + [vmem] * 3 + [hbm] * 6,
        out_specs=vmem,
        scratch_shapes=[
            pltpu.VMEM((adapters, rank, width), bf16),
            pltpu.VMEM(adapter_up_factor.shape, bf16),
            pltpu.VMEM((2, base, width), bf16),
            pltpu.VMEM((base, width), bf16),
            pltpu.VMEM((2, base, head_cols), bf16),
            pltpu.VMEM((base, head_cols), bf16),
            pltpu.VMEM((2, 8, 128), f32),
            pltpu.VMEM((2, 128, width), bf16),
            pltpu.VMEM((2,) + query_key_value_weight.shape, bf16),
            pltpu.VMEM((2,) + head_output_weight.shape, bf16),
            pltpu.VMEM((2,) + feedforward_weight.shape, bf16),
            pltpu.VMEM((own * n, piece, dh), bf16),
            pltpu.VMEM((n, 8, 128), jnp.int32),
            pltpu.SMEM((n, 8, 128), jnp.int32),
            pltpu.VMEM((n, 2, seqs, piece, dh), bf16),
            pltpu.VMEM((2, n, seqs, piece, dh), bf16),
            pltpu.VMEM((rows, wide), bf16),
            pltpu.VMEM((rows, wide), bf16),
            pltpu.VMEM((rows, wide), bf16),
            pltpu.VMEM((rows, wide), f32),
            pltpu.VMEM((rows, wide), f32),
            pltpu.VMEM((rows, wide), bf16),
            dma((n,)), dma((n,)), dma((n,)), dma((n,)), dma((2 * n,)), dma((2 * n,)),
            dma((10,)), dma((10,)), dma((8,)),
        ],
        compiler_params=pltpu.CompilerParams(
            collective_id=0, has_side_effects=True, vmem_limit_bytes=56 * 2**20),
        cost_estimate=pl.CostEstimate(flops=7 * 10**9, bytes_accessed=3 * 10**7, transcendentals=10**6),
    )(
        lengths, request_adapter_index, request_cache_index, decay_logit_bias, tokens, norm_gain_pair,
        head_gate_weight.transpose(0, 2, 1), adapter_down_factor.transpose(0, 2, 1), adapter_up_factor, query_key_value_weight,
        caches.reshape(own, n, piece, dh), head_output_weight, feedforward_weight,
    )
    return layer.astype(bf16)


def solution(mesh):
    placed = (
        P(("req", "col"), None),
        P(),
        P(None, None, "col"),
        P(None, None, "col"),
        P("col"),
        P("col", None, None),
        P(None, None, "col"),
        P("req", None, None),
        P("req", None),
        P("req", None),
        P("req", "col", None, None),
        P("col", None),
        P(None, None, "col"),
    )
    return jax.shard_map(
        on_device, mesh=mesh, in_specs=placed, out_specs=P(("req", "col"), None), check_vma=False
    )
```

```python
import functools
import math

import jax
import jax.numpy as jnp
from jax import lax
from jax.experimental import pallas as pl
from jax.experimental.pallas import tpu as pltpu
from jax.sharding import PartitionSpec as P

epsilon = 1e-05
MESH = pl.DeviceIdType.MESH


def mix_kernel(
    n, seqs, rank, half, dh,
    lens_ref, aidx_ref, cidx_ref, bias_ref, tok_ref, gain_ref, gate_ref, down_ref, up_ref,
    qkv_ref, cache_ref, wo_ref, ff_ref,
    out_ref,
    down_v, up_v, aux_s, auxr, upsel, upr, biasr, gates, wq, wo, wff, r1_0, r1_1, idxb, idxs, stage, r2,
    q_s, k_s, v_s, att_s, intra_s, head_s,
    s1, t1, si, ti, s2, t2, sp, tp, lsem,
):
    g = lax.axis_index("req")
    c = lax.axis_index("col")
    other = 1 - c
    r1 = (r1_0, r1_1)
    nh = n // 2
    start = (g // nh) * nh
    place = g - start
    own = cache_ref.shape[0]
    rows = tok_ref.shape[0]
    adapters = down_ref.shape[0]
    base = seqs * rank
    f32, bf16 = jnp.float32, jnp.bfloat16

    barrier = pltpu.get_barrier_semaphore()

    def hello(p, core):
        pl.semaphore_signal(barrier, inc=1, device_id=(p, core), device_id_type=MESH)

    def greet(k, carry):
        hello(lax.rem(g + k, n), c)
        return carry

    def greet_half(k, carry):
        hello(start + k, other)
        return carry

    lax.fori_loop(1, n, greet, 0)
    lax.fori_loop(0, nh, greet_half, 0)

    def local(src, dst, i):
        one = pltpu.make_async_copy(src, dst, lsem.at[i])
        one.start()
        return one

    local_down = local(down_ref, down_v, 0)
    local_up = local(up_ref, up_v, 1)
    local_c = [local(cache_ref.at[:, t, place], r1[t].at[pl.ds(own * g, own)], 8 + t) for t in range(2)]
    local_w = local(qkv_ref, wq.at[0], 3)
    local_wo = local(wo_ref, wo.at[0], 4)
    local_ff = local(ff_ref, wff.at[0], 5)

    lane8 = lax.broadcasted_iota(jnp.int32, (8, 128), 1)
    index = jnp.zeros((8, 128), jnp.int32)
    for s in range(2 * seqs):
        index = jnp.where(lane8 == s, cidx_ref[0, s], index)
    idxb[place] = index
    bias = jnp.zeros((8, 128), f32)
    for h in range(half):
        bias = jnp.where(lane8 == h, bias_ref[h], bias)
    biasr[0] = bias
    zeros = jnp.zeros((128 - 2 * half, gate_ref.shape[2]), f32)
    gates[0] = jnp.concatenate([gate_ref[0].astype(f32), gate_ref[1].astype(f32), zeros], axis=0).astype(bf16)

    pl.semaphore_wait(barrier, n - 1 + nh)

    def cache_copy(t, p, slot):
        return pltpu.make_async_remote_copy(
            src_ref=cache_ref.at[:, t, lax.rem(p, nh)], dst_ref=r1[t].at[pl.ds(own * slot, own)],
            send_sem=s1.at[t * n + p], recv_sem=t1.at[t * n + slot], device_id=(p, c), device_id_type=MESH)

    def index_copy(q, slot):
        return pltpu.make_async_remote_copy(
            src_ref=idxb.at[place], dst_ref=idxb.at[slot],
            send_sem=si.at[q], recv_sem=ti.at[slot], device_id=(start + q, c), device_id_type=MESH)

    def send_index(k, carry):
        index_copy(lax.rem(place + k, nh), place).start()
        return carry

    lax.fori_loop(1, nh, send_index, 0)
    for t in range(2):
        def first(k, carry, t=t):
            cache_copy(t, lax.rem(g + k, n), g).start()
            return carry

        lax.fori_loop(1, n, first, 0)

    pairs = []

    def pair(src, dst):
        i = len(pairs)
        one = pltpu.make_async_remote_copy(
            src_ref=src, dst_ref=dst, send_sem=sp.at[i], recv_sem=tp.at[i],
            device_id=(g, other), device_id_type=MESH)
        one.start()
        pairs.append(one)
        return one

    pair_gates = pair(gates.at[0], gates.at[1])
    pair_bias = pair(biasr.at[0], biasr.at[1])

    local_down.wait()
    local_up.wait()
    for b in range(2):
        for j in range(seqs):
            a = aidx_ref[0, b * seqs + j]
            mine_at = a - c * adapters
            held = (mine_at >= 0) & (mine_at < adapters)
            factor = down_v[jnp.clip(mine_at, 0, adapters - 1)]
            aux_s[b, j * rank:(j + 1) * rank, :] = jnp.where(held, factor, jnp.zeros_like(factor))
            upsel[b, j * rank:(j + 1) * rank, :] = up_v[a]
    pair_aux = pair(aux_s.at[other], auxr)
    pair_up = pair(upsel.at[other], upr)
    pair_w = pair(qkv_ref, wq.at[1])
    pair_wo = pair(wo_ref, wo.at[1])
    pair_ff = [pair(ff_ref.at[k], wff.at[1, k]) for k in range(3)]

    x = tok_ref[...].astype(f32)
    factor = lax.rsqrt(jnp.mean(x * x, axis=-1, keepdims=True) + epsilon)
    normed = (x * factor * gain_ref[0:1, :]).astype(bf16)

    ends = [lens_ref[0, c, 0]]
    for j in range(1, seqs - 1):
        ends.append(ends[-1] + lens_ref[0, c, j])

    def segment_of(shape, axis):
        pos = lax.broadcasted_iota(jnp.int32, shape, axis)
        seg = jnp.zeros(shape, jnp.int32)
        for e in ends:
            seg = seg + (pos >= e).astype(jnp.int32)
        return pos, seg

    q_pos, q_seg = segment_of((rows, rows), 0)
    k_pos, k_seg = segment_of((rows, rows), 1)
    allowed = (q_seg == k_seg) & (k_pos <= q_pos)
    _, seg_wide = segment_of((rows, 128), 0)
    _, seg_low = segment_of((rows, base), 0)

    local_w.wait()
    width = half * dh
    cols = pl.ds(0, width)
    own_q = jnp.dot(normed, wq[0, 0], preferred_element_type=f32)
    k_s[:, cols] = jnp.dot(normed, wq[0, 1], preferred_element_type=f32).astype(bf16)
    v_s[:, cols] = jnp.dot(normed, wq[0, 2], preferred_element_type=f32).astype(bf16)

    pair_gates.wait_recv()
    pair_bias.wait_recv()
    pair_aux.wait_recv()
    pair_up.wait_recv()
    nt = (((1,), (1,)), ((), ()))
    down = aux_s[c] + auxr[...]
    low = lax.dot_general(normed, down, nt, preferred_element_type=f32)
    lane = lax.broadcasted_iota(jnp.int32, (rows, base), 1)
    low = jnp.where(lane // rank == seg_low, low, 0.0).astype(bf16)
    own_q = own_q + jnp.dot(low, upsel[c], preferred_element_type=f32)
    q_s[:, cols] = own_q.astype(bf16)

    ones = allowed.astype(f32).astype(bf16)
    levels, levels_t, mixes = [], [], []
    for b in range(2):
        terms = lax.dot_general(normed, gates[b], nt, preferred_element_type=f32)
        shifted = terms + biasr[b][0:1, :]
        log_keep = jnp.minimum(shifted, 0.0) - jnp.log1p(jnp.exp(-jnp.abs(shifted)))
        mixes.append(1.0 / (1.0 + jnp.exp(-terms)))
        part = log_keep.astype(bf16)
        level = jnp.dot(ones, part, preferred_element_type=f32)
        rest = log_keep - part.astype(f32)
        part = rest.astype(bf16)
        level = level + jnp.dot(ones, part, preferred_element_type=f32)
        part = (rest - part.astype(f32)).astype(bf16)
        level = level + jnp.dot(ones, part, preferred_element_type=f32)
        levels.append(level)
        levels_t.append(jnp.transpose(level))

    def index_wait(k, carry):
        q = lax.rem(place + k, nh)
        index_copy(q, q).wait_recv()
        return carry

    def pick(t, q):
        for b in range(2):
            for j in range(seqs):
                i = idxs[q, 0, b * seqs + j]
                piece = r1[t][jnp.minimum(i, own * n - 1)]
                stage[t, q, b, j] = jnp.where(i < own * n, piece, jnp.zeros_like(piece))

    def second_copy(t, q, core, slot, at):
        return pltpu.make_async_remote_copy(
            src_ref=stage.at[t, q, core], dst_ref=r2.at[t, slot, at],
            send_sem=s2.at[(t * nh + q) * 2 + core], recv_sem=t2.at[(t * 2 + slot) * nh + at],
            device_id=(start + q, core), device_id_type=MESH)

    def second_step(t):
        local_c[t].wait()

        def first_wait(k, carry):
            p = lax.rem(g + k, n)
            cache_copy(t, p, p).wait_recv()
            return carry

        lax.fori_loop(1, n, first_wait, 0)

        def second(k, carry):
            q = lax.rem(place + k, nh)
            pick(t, q)
            second_copy(t, q, c, 0, place).start()
            second_copy(t, q, other, 1, place).start()
            return carry

        lax.fori_loop(1, nh, second, 0)
        pick(t, place)
        second_copy(t, place, other, 1, place).start()
        return local(stage.at[t, place, c], r2.at[t, 0, place], 6 + t)

    def second_wait(t):
        def one(k, carry):
            q = lax.rem(place + k, nh)
            second_copy(t, q, c, 0, q).wait_recv()
            second_copy(t, q, other, 1, q).wait_recv()
            return carry

        lax.fori_loop(1, nh, one, 0)
        second_copy(t, place, other, 1, place).wait_recv()
        keep[t].wait()

    lax.fori_loop(1, nh, index_wait, 0)
    local(idxb, idxs, 2).wait()
    keep = [second_step(0)]

    scale = 1.0 / math.sqrt(dh)

    def attend(h):
        cols = pl.ds(h * dh, dh)
        b, i = h // half, h % half
        scores = lax.dot_general(q_s[:, cols], k_s[:, cols], nt, preferred_element_type=f32) * scale
        masked = jnp.where(allowed, scores, -jnp.inf)
        peak = jnp.max(masked, axis=1, keepdims=True)
        weights = jnp.exp(masked - peak)
        probs = (weights * (1.0 / jnp.sum(weights, axis=1, keepdims=True))).astype(bf16)
        att_s[:, cols] = jnp.dot(probs, v_s[:, cols], preferred_element_type=f32)
        gap = jnp.where(allowed, levels[b][:, i:i + 1] - levels_t[b][i:i + 1, :], -jnp.inf)
        memory_w = (scores * jnp.exp(gap)).astype(bf16)
        intra_s[:, cols] = jnp.dot(memory_w, v_s[:, cols], preferred_element_type=f32)

    for h in range(half):
        attend(h)
    pair_w.wait_recv()
    cols = pl.ds(width, width)
    q = jnp.dot(normed, wq[1, 0], preferred_element_type=f32)
    q_s[:, cols] = (q + jnp.dot(low, upr[...], preferred_element_type=f32)).astype(bf16)
    k_s[:, cols] = jnp.dot(normed, wq[1, 1], preferred_element_type=f32).astype(bf16)
    v_s[:, cols] = jnp.dot(normed, wq[1, 2], preferred_element_type=f32).astype(bf16)
    for h in range(half, half + half // 2):
        attend(h)
    keep.append(second_step(1))
    for h in range(half + half // 2, 2 * half):
        attend(h)

    per_head = 2 * nh // half

    def recall(b, i):
        h = b * half + i
        t, at = i // (half // 2), (i % (half // 2)) * per_head
        cols = pl.ds(h * dh, dh)
        q = q_s[:, cols]
        carried = jnp.zeros((rows, dh), f32)
        for j in range(seqs):
            state = r2[t, b, at:at + per_head, j]
            state = state.astype(f32).reshape(dh, dh).astype(bf16)
            carried = jnp.where(seg_wide == j, jnp.dot(q, state, preferred_element_type=f32), carried)
        recalled = carried * jnp.exp(levels[b][:, i:i + 1]) + intra_s[:, cols]
        factor = lax.rsqrt(jnp.mean(recalled * recalled, axis=1, keepdims=True) + epsilon)
        head_s[:, cols] = (att_s[:, cols] + mixes[b][:, half + i:half + i + 1] * recalled * factor).astype(bf16)

    for t in range(2):
        second_wait(t)
        for b in range(2):
            for i in range(t * (half // 2), (t + 1) * (half // 2)):
                recall(b, i)

    local_wo.wait()
    pair_wo.wait_recv()
    proj = jnp.dot(head_s[:, :width], wo[0], preferred_element_type=f32)
    proj = proj + jnp.dot(head_s[:, width:], wo[1], preferred_element_type=f32)
    mixed = (tok_ref[...].astype(f32) + proj).astype(bf16).astype(f32)
    factor = lax.rsqrt(jnp.mean(mixed * mixed, axis=-1, keepdims=True) + epsilon)
    normed_two = (mixed * factor * gain_ref[1:2, :]).astype(bf16)
    local_ff.wait()
    for b in range(2):
        if b == 1:
            pair_ff[0].wait_recv()
        gate = jnp.dot(normed_two, wff[b, 0], preferred_element_type=f32)
        if b == 1:
            pair_ff[1].wait_recv()
        upper = jnp.dot(normed_two, wff[b, 1], preferred_element_type=f32)
        hidden = (gate / (1.0 + jnp.exp(-gate)) * upper).astype(bf16)
        if b == 1:
            pair_ff[2].wait_recv()
        down_t = lax.dot_general(wff[b, 2], hidden, nt, preferred_element_type=f32)
        feed_t = down_t if b == 0 else feed_t + down_t
    out_ref[...] = (mixed + jnp.transpose(feed_t)).astype(bf16)

    def drain_first(k, carry):
        p = lax.rem(g + k, n)
        cache_copy(0, p, g).wait_send()
        cache_copy(1, p, g).wait_send()
        return carry

    def drain_second(k, carry):
        q = lax.rem(place + k, nh)
        index_copy(q, place).wait_send()
        for t in range(2):
            second_copy(t, q, c, 0, place).wait_send()
            second_copy(t, q, other, 1, place).wait_send()
        return carry

    lax.fori_loop(1, n, drain_first, 0)
    lax.fori_loop(1, nh, drain_second, 0)
    for t in range(2):
        second_copy(t, place, other, 1, place).wait_send()
    for one in pairs:
        one.wait_send()


def on_device(
    tokens, norm_gain_pair, query_key_value_weight, head_gate_weight, decay_logit_bias,
    adapter_down_factor, adapter_up_factor, lengths, request_adapter_index, request_cache_index,
    caches, head_output_weight, feedforward_weight,
):
    n = lax.axis_size("req")
    rows, width = tokens.shape
    seqs = lengths.shape[2]
    adapters, _, rank = adapter_down_factor.shape
    half = head_gate_weight.shape[2]
    head_cols = query_key_value_weight.shape[2]
    dh = head_cols // half
    own = caches.shape[0]
    nh = n // 2
    piece = half * dh // n
    base = seqs * rank
    bf16, f32 = jnp.bfloat16, jnp.float32

    vmem = pl.BlockSpec(memory_space=pltpu.VMEM)
    smem = pl.BlockSpec(memory_space=pltpu.SMEM)
    hbm = pl.BlockSpec(memory_space=pl.ANY)
    dma = pltpu.SemaphoreType.DMA
    wide = 2 * head_cols
    return pl.pallas_call(
        functools.partial(mix_kernel, n, seqs, rank, half, dh),
        out_shape=jax.ShapeDtypeStruct((rows, width), bf16),
        in_specs=[smem] * 4 + [vmem] * 3 + [hbm] * 6,
        out_specs=vmem,
        scratch_shapes=[
            pltpu.VMEM((adapters, rank, width), bf16),
            pltpu.VMEM(adapter_up_factor.shape, bf16),
            pltpu.VMEM((2, base, width), bf16),
            pltpu.VMEM((base, width), bf16),
            pltpu.VMEM((2, base, head_cols), bf16),
            pltpu.VMEM((base, head_cols), bf16),
            pltpu.VMEM((2, 8, 128), f32),
            pltpu.VMEM((2, 128, width), bf16),
            pltpu.VMEM((2,) + query_key_value_weight.shape, bf16),
            pltpu.VMEM((2,) + head_output_weight.shape, bf16),
            pltpu.VMEM((2,) + feedforward_weight.shape, bf16),
            pltpu.VMEM((own * n, piece, dh), bf16),
            pltpu.VMEM((own * n, piece, dh), bf16),
            pltpu.VMEM((nh, 8, 128), jnp.int32),
            pltpu.SMEM((nh, 8, 128), jnp.int32),
            pltpu.VMEM((2, nh, 2, seqs, piece, dh), bf16),
            pltpu.VMEM((2, 2, nh, seqs, piece, dh), bf16),
            pltpu.VMEM((rows, wide), bf16),
            pltpu.VMEM((rows, wide), bf16),
            pltpu.VMEM((rows, wide), bf16),
            pltpu.VMEM((rows, wide), f32),
            pltpu.VMEM((rows, wide), f32),
            pltpu.VMEM((rows, wide), bf16),
            dma((2 * n,)), dma((2 * n,)), dma((nh,)), dma((nh,)), dma((4 * nh,)), dma((4 * nh,)),
            dma((10,)), dma((10,)), dma((10,)),
        ],
        compiler_params=pltpu.CompilerParams(
            collective_id=0, has_side_effects=True, vmem_limit_bytes=56 * 2**20),
        cost_estimate=pl.CostEstimate(flops=7 * 10**9, bytes_accessed=3 * 10**7, transcendentals=10**6),
    )(
        lengths, request_adapter_index, request_cache_index, decay_logit_bias, tokens, norm_gain_pair,
        head_gate_weight.transpose(0, 2, 1), adapter_down_factor.transpose(0, 2, 1), adapter_up_factor, query_key_value_weight,
        caches.reshape(own, 2, nh, piece, dh), head_output_weight, feedforward_weight,
    )


def solution(mesh):
    placed = (
        P(("req", "col"), None),
        P(),
        P(None, None, "col"),
        P(None, None, "col"),
        P("col"),
        P("col", None, None),
        P(None, None, "col"),
        P("req", None, None),
        P("req", None),
        P("req", None),
        P("req", "col", None, None),
        P("col", None),
        P(None, None, "col"),
    )
    return jax.shard_map(
        on_device, mesh=mesh, in_specs=placed, out_specs=P(("req", "col"), None), check_vma=False
    )
```

```python
import functools
import math

import jax
import jax.numpy as jnp
from jax import lax
from jax.experimental import pallas as pl
from jax.experimental.pallas import tpu as pltpu
from jax.sharding import PartitionSpec as P

epsilon = 1e-05
MESH = pl.DeviceIdType.MESH


def mix_kernel(
    n, seqs, rank, half, dh,
    lens_ref, aidx_ref, cidx_ref, bias_ref, tok_ref, gain_ref, gate_ref, down_ref, up_ref,
    qkv_ref, cache_ref, wo_ref, ff_ref,
    out_ref,
    down_v, up_v, aux_s, auxr, upsel, upr, biasr, gates, wq, wo, wff, r1_0, r1_1, idxb, idxs, stage, r2,
    q_s, k_s, v_s, att_s, intra_s, head_s,
    s1, t1, si, ti, s2, t2, sp, tp, lsem,
):
    g = lax.axis_index("req")
    c = lax.axis_index("col")
    other = 1 - c
    r1 = (r1_0, r1_1)
    nh = n // 2
    start = (g // nh) * nh
    place = g - start
    own = cache_ref.shape[0]
    rows = tok_ref.shape[0]
    adapters = down_ref.shape[0]
    base = seqs * rank
    f32, bf16 = jnp.float32, jnp.bfloat16

    barrier = pltpu.get_barrier_semaphore()

    def hello(p, core):
        pl.semaphore_signal(barrier, inc=1, device_id=(p, core), device_id_type=MESH)

    def greet(k, carry):
        hello(lax.rem(g + k, n), c)
        return carry

    def greet_half(k, carry):
        hello(start + k, other)
        return carry

    lax.fori_loop(1, n, greet, 0)
    lax.fori_loop(0, nh, greet_half, 0)

    def local(src, dst, i):
        one = pltpu.make_async_copy(src, dst, lsem.at[i])
        one.start()
        return one

    local_down = local(down_ref, down_v, 0)
    local_up = local(up_ref, up_v, 1)
    local_c = [local(cache_ref.at[:, t, place], r1[t].at[pl.ds(own * g, own)], 8 + t) for t in range(2)]
    local_w = local(qkv_ref, wq.at[0], 3)
    local_wo = local(wo_ref, wo.at[0], 4)
    local_ff = local(ff_ref, wff.at[0], 5)

    lane8 = lax.broadcasted_iota(jnp.int32, (8, 128), 1)
    index = jnp.zeros((8, 128), jnp.int32)
    for s in range(2 * seqs):
        index = jnp.where(lane8 == s, cidx_ref[0, s], index)
    idxb[place] = index
    bias = jnp.zeros((8, 128), f32)
    for h in range(half):
        bias = jnp.where(lane8 == h, bias_ref[h], bias)
    biasr[0] = bias
    zeros = jnp.zeros((128 - 2 * half, gate_ref.shape[2]), f32)
    gates[0] = jnp.concatenate([gate_ref[0].astype(f32), gate_ref[1].astype(f32), zeros], axis=0).astype(bf16)

    pl.semaphore_wait(barrier, n - 1 + nh)

    def cache_copy(t, p, slot):
        return pltpu.make_async_remote_copy(
            src_ref=cache_ref.at[:, t, lax.rem(p, nh)], dst_ref=r1[t].at[pl.ds(own * slot, own)],
            send_sem=s1.at[t * n + p], recv_sem=t1.at[t * n + slot], device_id=(p, c), device_id_type=MESH)

    def index_copy(q, slot):
        return pltpu.make_async_remote_copy(
            src_ref=idxb.at[place], dst_ref=idxb.at[slot],
            send_sem=si.at[q], recv_sem=ti.at[slot], device_id=(start + q, c), device_id_type=MESH)

    def send_index(k, carry):
        index_copy(lax.rem(place + k, nh), place).start()
        return carry

    lax.fori_loop(1, nh, send_index, 0)
    for t in range(2):
        def first(k, carry, t=t):
            cache_copy(t, lax.rem(g + k, n), g).start()
            return carry

        lax.fori_loop(1, n, first, 0)

    pairs = []

    def pair(src, dst):
        i = len(pairs)
        one = pltpu.make_async_remote_copy(
            src_ref=src, dst_ref=dst, send_sem=sp.at[i], recv_sem=tp.at[i],
            device_id=(g, other), device_id_type=MESH)
        one.start()
        pairs.append(one)
        return one

    pair_gates = pair(gates.at[0], gates.at[1])
    pair_bias = pair(biasr.at[0], biasr.at[1])

    local_down.wait()
    local_up.wait()
    for b in range(2):
        for j in range(seqs):
            a = aidx_ref[0, b * seqs + j]
            mine_at = a - c * adapters
            held = (mine_at >= 0) & (mine_at < adapters)
            factor = down_v[jnp.clip(mine_at, 0, adapters - 1)]
            aux_s[b, j * rank:(j + 1) * rank, :] = jnp.where(held, factor, jnp.zeros_like(factor))
            upsel[b, j * rank:(j + 1) * rank, :] = up_v[a]
    pair_aux = pair(aux_s.at[other], auxr)
    pair_up = pair(upsel.at[other], upr)
    pair_w = pair(qkv_ref, wq.at[1])
    pair_wo = pair(wo_ref, wo.at[1])
    pair_ff = [pair(ff_ref.at[k], wff.at[1, k]) for k in range(3)]

    x = tok_ref[...].astype(f32)
    factor = lax.rsqrt(jnp.mean(x * x, axis=-1, keepdims=True) + epsilon)
    normed = (x * factor * gain_ref[0:1, :]).astype(bf16)

    ends = [lens_ref[0, c, 0]]
    for j in range(1, seqs - 1):
        ends.append(ends[-1] + lens_ref[0, c, j])

    def segment_of(shape, axis):
        pos = lax.broadcasted_iota(jnp.int32, shape, axis)
        seg = jnp.zeros(shape, jnp.int32)
        for e in ends:
            seg = seg + (pos >= e).astype(jnp.int32)
        return pos, seg

    q_pos, q_seg = segment_of((rows, rows), 0)
    k_pos, k_seg = segment_of((rows, rows), 1)
    allowed = (q_seg == k_seg) & (k_pos <= q_pos)
    _, seg_wide = segment_of((rows, 128), 0)
    _, seg_low = segment_of((rows, base), 0)

    local_w.wait()
    width = half * dh
    cols = pl.ds(0, width)
    own_q = jnp.dot(normed, wq[0, 0], preferred_element_type=f32)
    k_s[:, cols] = jnp.dot(normed, wq[0, 1], preferred_element_type=f32).astype(bf16)
    v_s[:, cols] = jnp.dot(normed, wq[0, 2], preferred_element_type=f32).astype(bf16)

    pair_gates.wait_recv()
    pair_bias.wait_recv()
    pair_aux.wait_recv()
    pair_up.wait_recv()
    nt = (((1,), (1,)), ((), ()))
    down = aux_s[c] + auxr[...]
    low = lax.dot_general(normed, down, nt, preferred_element_type=f32)
    lane = lax.broadcasted_iota(jnp.int32, (rows, base), 1)
    low = jnp.where(lane // rank == seg_low, low, 0.0).astype(bf16)
    own_q = own_q + jnp.dot(low, upsel[c], preferred_element_type=f32)
    q_s[:, cols] = own_q.astype(bf16)

    ones = allowed.astype(f32).astype(bf16)
    levels, levels_t, mixes = [], [], []
    for b in range(2):
        terms = lax.dot_general(normed, gates[b], nt, preferred_element_type=f32)
        shifted = terms + biasr[b][0:1, :]
        log_keep = jnp.minimum(shifted, 0.0) - jnp.log1p(jnp.exp(-jnp.abs(shifted)))
        mixes.append(1.0 / (1.0 + jnp.exp(-terms)))
        part = log_keep.astype(bf16)
        level = jnp.dot(ones, part, preferred_element_type=f32)
        rest = log_keep - part.astype(f32)
        part = rest.astype(bf16)
        level = level + jnp.dot(ones, part, preferred_element_type=f32)
        part = (rest - part.astype(f32)).astype(bf16)
        level = level + jnp.dot(ones, part, preferred_element_type=f32)
        levels.append(level)
        levels_t.append(jnp.transpose(level))

    def index_wait(k, carry):
        q = lax.rem(place + k, nh)
        index_copy(q, q).wait_recv()
        return carry

    def pick(t, q):
        for b in range(2):
            for j in range(seqs):
                i = idxs[q, 0, b * seqs + j]
                piece = r1[t][jnp.minimum(i, own * n - 1)]
                stage[t, q, b, j] = jnp.where(i < own * n, piece, jnp.zeros_like(piece))

    def second_copy(t, q, core, slot, at):
        return pltpu.make_async_remote_copy(
            src_ref=stage.at[t, q, core], dst_ref=r2.at[t, slot, at],
            send_sem=s2.at[(t * nh + q) * 2 + core], recv_sem=t2.at[(t * 2 + slot) * nh + at],
            device_id=(start + q, core), device_id_type=MESH)

    def second_step(t):
        local_c[t].wait()

        def first_wait(k, carry):
            p = lax.rem(g + k, n)
            cache_copy(t, p, p).wait_recv()
            return carry

        lax.fori_loop(1, n, first_wait, 0)

        def second(k, carry):
            q = lax.rem(place + k, nh)
            pick(t, q)
            second_copy(t, q, c, 0, place).start()
            second_copy(t, q, other, 1, place).start()
            return carry

        lax.fori_loop(1, nh, second, 0)
        pick(t, place)
        second_copy(t, place, other, 1, place).start()
        return local(stage.at[t, place, c], r2.at[t, 0, place], 6 + t)

    def second_wait(t):
        def one(k, carry):
            q = lax.rem(place + k, nh)
            second_copy(t, q, c, 0, q).wait_recv()
            second_copy(t, q, other, 1, q).wait_recv()
            return carry

        lax.fori_loop(1, nh, one, 0)
        second_copy(t, place, other, 1, place).wait_recv()
        keep[t].wait()

    lax.fori_loop(1, nh, index_wait, 0)
    local(idxb, idxs, 2).wait()
    keep = [second_step(0)]

    scale = 1.0 / math.sqrt(dh)

    def attend(h):
        cols = pl.ds(h * dh, dh)
        b, i = h // half, h % half
        scores = lax.dot_general(q_s[:, cols], k_s[:, cols], nt, preferred_element_type=f32) * scale
        masked = jnp.where(allowed, scores, -jnp.inf)
        peak = jnp.max(masked, axis=1, keepdims=True)
        weights = jnp.exp(masked - peak)
        probs = (weights * (1.0 / jnp.sum(weights, axis=1, keepdims=True))).astype(bf16)
        att_s[:, cols] = jnp.dot(probs, v_s[:, cols], preferred_element_type=f32)
        gap = jnp.where(allowed, levels[b][:, i:i + 1] - levels_t[b][i:i + 1, :], -jnp.inf)
        memory_w = (scores * jnp.exp(gap)).astype(bf16)
        intra_s[:, cols] = jnp.dot(memory_w, v_s[:, cols], preferred_element_type=f32)

    for h in range(half):
        attend(h)
    pair_w.wait_recv()
    cols = pl.ds(width, width)
    q = jnp.dot(normed, wq[1, 0], preferred_element_type=f32)
    q_s[:, cols] = (q + jnp.dot(low, upr[...], preferred_element_type=f32)).astype(bf16)
    k_s[:, cols] = jnp.dot(normed, wq[1, 1], preferred_element_type=f32).astype(bf16)
    v_s[:, cols] = jnp.dot(normed, wq[1, 2], preferred_element_type=f32).astype(bf16)
    keep.append(second_step(1))
    for h in range(half, 2 * half):
        attend(h)

    per_head = 2 * nh // half

    def recall(b, i):
        h = b * half + i
        t, at = i // (half // 2), (i % (half // 2)) * per_head
        cols = pl.ds(h * dh, dh)
        q = q_s[:, cols]
        carried = jnp.zeros((rows, dh), f32)
        for j in range(seqs):
            state = r2[t, b, at:at + per_head, j]
            state = state.astype(f32).reshape(dh, dh).astype(bf16)
            carried = jnp.where(seg_wide == j, jnp.dot(q, state, preferred_element_type=f32), carried)
        recalled = carried * jnp.exp(levels[b][:, i:i + 1]) + intra_s[:, cols]
        factor = lax.rsqrt(jnp.mean(recalled * recalled, axis=1, keepdims=True) + epsilon)
        head_s[:, cols] = (att_s[:, cols] + mixes[b][:, half + i:half + i + 1] * recalled * factor).astype(bf16)

    for t in range(2):
        second_wait(t)
        for b in range(2):
            for i in range(t * (half // 2), (t + 1) * (half // 2)):
                recall(b, i)

    local_wo.wait()
    pair_wo.wait_recv()
    proj = jnp.dot(head_s[:, :width], wo[0], preferred_element_type=f32)
    proj = proj + jnp.dot(head_s[:, width:], wo[1], preferred_element_type=f32)
    mixed = (tok_ref[...].astype(f32) + proj).astype(bf16).astype(f32)
    factor = lax.rsqrt(jnp.mean(mixed * mixed, axis=-1, keepdims=True) + epsilon)
    normed_two = (mixed * factor * gain_ref[1:2, :]).astype(bf16)
    local_ff.wait()
    for b in range(2):
        if b == 1:
            pair_ff[0].wait_recv()
        gate = jnp.dot(normed_two, wff[b, 0], preferred_element_type=f32)
        if b == 1:
            pair_ff[1].wait_recv()
        upper = jnp.dot(normed_two, wff[b, 1], preferred_element_type=f32)
        hidden = (gate / (1.0 + jnp.exp(-gate)) * upper).astype(bf16)
        if b == 1:
            pair_ff[2].wait_recv()
        down_t = lax.dot_general(wff[b, 2], hidden, nt, preferred_element_type=f32)
        feed_t = down_t if b == 0 else feed_t + down_t
    out_ref[...] = (mixed + jnp.transpose(feed_t)).astype(bf16)

    def drain_first(k, carry):
        p = lax.rem(g + k, n)
        cache_copy(0, p, g).wait_send()
        cache_copy(1, p, g).wait_send()
        return carry

    def drain_second(k, carry):
        q = lax.rem(place + k, nh)
        index_copy(q, place).wait_send()
        for t in range(2):
            second_copy(t, q, c, 0, place).wait_send()
            second_copy(t, q, other, 1, place).wait_send()
        return carry

    lax.fori_loop(1, n, drain_first, 0)
    lax.fori_loop(1, nh, drain_second, 0)
    for t in range(2):
        second_copy(t, place, other, 1, place).wait_send()
    for one in pairs:
        one.wait_send()


def on_device(
    tokens, norm_gain_pair, query_key_value_weight, head_gate_weight, decay_logit_bias,
    adapter_down_factor, adapter_up_factor, lengths, request_adapter_index, request_cache_index,
    caches, head_output_weight, feedforward_weight,
):
    n = lax.axis_size("req")
    rows, width = tokens.shape
    seqs = lengths.shape[2]
    adapters, _, rank = adapter_down_factor.shape
    half = head_gate_weight.shape[2]
    head_cols = query_key_value_weight.shape[2]
    dh = head_cols // half
    own = caches.shape[0]
    nh = n // 2
    piece = half * dh // n
    base = seqs * rank
    bf16, f32 = jnp.bfloat16, jnp.float32

    vmem = pl.BlockSpec(memory_space=pltpu.VMEM)
    smem = pl.BlockSpec(memory_space=pltpu.SMEM)
    hbm = pl.BlockSpec(memory_space=pl.ANY)
    dma = pltpu.SemaphoreType.DMA
    wide = 2 * head_cols
    return pl.pallas_call(
        functools.partial(mix_kernel, n, seqs, rank, half, dh),
        out_shape=jax.ShapeDtypeStruct((rows, width), bf16),
        in_specs=[smem] * 4 + [vmem] * 3 + [hbm] * 6,
        out_specs=vmem,
        scratch_shapes=[
            pltpu.VMEM((adapters, rank, width), bf16),
            pltpu.VMEM(adapter_up_factor.shape, bf16),
            pltpu.VMEM((2, base, width), bf16),
            pltpu.VMEM((base, width), bf16),
            pltpu.VMEM((2, base, head_cols), bf16),
            pltpu.VMEM((base, head_cols), bf16),
            pltpu.VMEM((2, 8, 128), f32),
            pltpu.VMEM((2, 128, width), bf16),
            pltpu.VMEM((2,) + query_key_value_weight.shape, bf16),
            pltpu.VMEM((2,) + head_output_weight.shape, bf16),
            pltpu.VMEM((2,) + feedforward_weight.shape, bf16),
            pltpu.VMEM((own * n, piece, dh), bf16),
            pltpu.VMEM((own * n, piece, dh), bf16),
            pltpu.VMEM((nh, 8, 128), jnp.int32),
            pltpu.SMEM((nh, 8, 128), jnp.int32),
            pltpu.VMEM((2, nh, 2, seqs, piece, dh), bf16),
            pltpu.VMEM((2, 2, nh, seqs, piece, dh), bf16),
            pltpu.VMEM((rows, wide), bf16),
            pltpu.VMEM((rows, wide), bf16),
            pltpu.VMEM((rows, wide), bf16),
            pltpu.VMEM((rows, wide), f32),
            pltpu.VMEM((rows, wide), f32),
            pltpu.VMEM((rows, wide), bf16),
            dma((2 * n,)), dma((2 * n,)), dma((nh,)), dma((nh,)), dma((4 * nh,)), dma((4 * nh,)),
            dma((10,)), dma((10,)), dma((10,)),
        ],
        compiler_params=pltpu.CompilerParams(
            collective_id=0, has_side_effects=True, vmem_limit_bytes=56 * 2**20),
        cost_estimate=pl.CostEstimate(flops=7 * 10**9, bytes_accessed=3 * 10**7, transcendentals=10**6),
    )(
        lengths, request_adapter_index, request_cache_index, decay_logit_bias, tokens, norm_gain_pair,
        head_gate_weight.transpose(0, 2, 1), adapter_down_factor.transpose(0, 2, 1), adapter_up_factor, query_key_value_weight,
        caches.reshape(own, 2, nh, piece, dh), head_output_weight, feedforward_weight,
    )


def solution(mesh):
    placed = (
        P(("req", "col"), None),
        P(),
        P(None, None, "col"),
        P(None, None, "col"),
        P("col"),
        P("col", None, None),
        P(None, None, "col"),
        P("req", None, None),
        P("req", None),
        P("req", None),
        P("req", "col", None, None),
        P("col", None),
        P(None, None, "col"),
    )
    return jax.shard_map(
        on_device, mesh=mesh, in_specs=placed, out_specs=P(("req", "col"), None), check_vma=False
    )
```

```python
import functools
import math

import jax
import jax.numpy as jnp
from jax import lax
from jax.experimental import pallas as pl
from jax.experimental.pallas import tpu as pltpu
from jax.sharding import PartitionSpec as P

epsilon = 1e-05
MESH = pl.DeviceIdType.MESH


def mix_kernel(
    n, seqs, rank, half, dh,
    lens_ref, aidx_ref, cidx_ref, bias_ref, tok_ref, gain_ref, gate_ref, down_ref, up_ref,
    qkv_ref, cache_ref, wo_ref, ff_ref,
    out_ref,
    down_v, up_v, aux_s, auxr, upsel, upr, biasr, gates, wq, wo, wff, r1_0, r1_1, idxb, idxs, stage, r2,
    q_s, k_s, v_s, att_s, intra_s, head_s,
    s1, t1, si, ti, s2, t2, sp, tp, lsem,
):
    g = lax.axis_index("req")
    c = lax.axis_index("col")
    other = 1 - c
    r1 = (r1_0, r1_1)
    nh = n // 2
    start = (g // nh) * nh
    place = g - start
    own = cache_ref.shape[0]
    rows = tok_ref.shape[0]
    adapters = down_ref.shape[0]
    base = seqs * rank
    f32, bf16 = jnp.float32, jnp.bfloat16

    barrier = pltpu.get_barrier_semaphore()

    def hello(p, core):
        pl.semaphore_signal(barrier, inc=1, device_id=(p, core), device_id_type=MESH)

    def greet(k, carry):
        hello(lax.rem(g + k, n), c)
        return carry

    def greet_half(k, carry):
        hello(start + k, other)
        return carry

    lax.fori_loop(1, n, greet, 0)
    lax.fori_loop(0, nh, greet_half, 0)

    def local(src, dst, i):
        one = pltpu.make_async_copy(src, dst, lsem.at[i])
        one.start()
        return one

    local_down = local(down_ref, down_v, 0)
    local_up = local(up_ref, up_v, 1)
    local_c = [local(cache_ref.at[:, t, place], r1[t].at[pl.ds(own * g, own)], 8 + t) for t in range(2)]
    local_w = local(qkv_ref, wq.at[0], 3)
    local_wo = local(wo_ref, wo.at[0], 4)
    local_ff = local(ff_ref, wff.at[0], 5)

    lane8 = lax.broadcasted_iota(jnp.int32, (8, 128), 1)
    index = jnp.zeros((8, 128), jnp.int32)
    for s in range(2 * seqs):
        index = jnp.where(lane8 == s, cidx_ref[0, s], index)
    idxb[place] = index
    bias = jnp.zeros((8, 128), f32)
    for h in range(half):
        bias = jnp.where(lane8 == h, bias_ref[h], bias)
    biasr[0] = bias
    zeros = jnp.zeros((128 - 2 * half, gate_ref.shape[2]), f32)
    gates[0] = jnp.concatenate([gate_ref[0].astype(f32), gate_ref[1].astype(f32), zeros], axis=0).astype(bf16)

    pl.semaphore_wait(barrier, n - 1 + nh)

    def cache_copy(t, p, slot):
        return pltpu.make_async_remote_copy(
            src_ref=cache_ref.at[:, t, lax.rem(p, nh)], dst_ref=r1[t].at[pl.ds(own * slot, own)],
            send_sem=s1.at[t * n + p], recv_sem=t1.at[t * n + slot], device_id=(p, c), device_id_type=MESH)

    def index_copy(q, slot):
        return pltpu.make_async_remote_copy(
            src_ref=idxb.at[place], dst_ref=idxb.at[slot],
            send_sem=si.at[q], recv_sem=ti.at[slot], device_id=(start + q, c), device_id_type=MESH)

    def send_index(k, carry):
        index_copy(lax.rem(place + k, nh), place).start()
        return carry

    lax.fori_loop(1, nh, send_index, 0)
    for t in range(2):
        def first(k, carry, t=t):
            cache_copy(t, lax.rem(g + k, n), g).start()
            return carry

        lax.fori_loop(1, n, first, 0)

    pairs = []

    def pair(src, dst):
        i = len(pairs)
        one = pltpu.make_async_remote_copy(
            src_ref=src, dst_ref=dst, send_sem=sp.at[i], recv_sem=tp.at[i],
            device_id=(g, other), device_id_type=MESH)
        one.start()
        pairs.append(one)
        return one

    pair_gates = pair(gates.at[0], gates.at[1])
    pair_bias = pair(biasr.at[0], biasr.at[1])

    local_down.wait()
    local_up.wait()
    for b in range(2):
        for j in range(seqs):
            a = aidx_ref[0, b * seqs + j]
            mine_at = a - c * adapters
            held = (mine_at >= 0) & (mine_at < adapters)
            factor = down_v[jnp.clip(mine_at, 0, adapters - 1)]
            aux_s[b, j * rank:(j + 1) * rank, :] = jnp.where(held, factor, jnp.zeros_like(factor))
            upsel[b, j * rank:(j + 1) * rank, :] = up_v[a]
    pair_aux = pair(aux_s.at[other], auxr)
    pair_up = pair(upsel.at[other], upr)
    pair_w = pair(qkv_ref, wq.at[1])
    pair_wo = pair(wo_ref, wo.at[1])
    pair_ff = [pair(ff_ref.at[k], wff.at[1, k]) for k in range(3)]

    x = tok_ref[...].astype(f32)
    factor = lax.rsqrt(jnp.mean(x * x, axis=-1, keepdims=True) + epsilon)
    normed = (x * factor * gain_ref[0:1, :]).astype(bf16)

    ends = [lens_ref[0, c, 0]]
    for j in range(1, seqs - 1):
        ends.append(ends[-1] + lens_ref[0, c, j])

    def segment_of(shape, axis):
        pos = lax.broadcasted_iota(jnp.int32, shape, axis)
        seg = jnp.zeros(shape, jnp.int32)
        for e in ends:
            seg = seg + (pos >= e).astype(jnp.int32)
        return pos, seg

    q_pos, q_seg = segment_of((rows, rows), 0)
    k_pos, k_seg = segment_of((rows, rows), 1)
    allowed = (q_seg == k_seg) & (k_pos <= q_pos)
    _, seg_wide = segment_of((rows, 128), 0)
    _, seg_low = segment_of((rows, base), 0)

    local_w.wait()
    width = half * dh
    cols = pl.ds(0, width)
    own_q = jnp.dot(normed, wq[0, 0], preferred_element_type=f32)
    k_s[:, cols] = jnp.dot(normed, wq[0, 1], preferred_element_type=f32).astype(bf16)
    v_s[:, cols] = jnp.dot(normed, wq[0, 2], preferred_element_type=f32).astype(bf16)

    pair_gates.wait_recv()
    pair_bias.wait_recv()
    pair_aux.wait_recv()
    pair_up.wait_recv()
    nt = (((1,), (1,)), ((), ()))
    down = aux_s[c] + auxr[...]
    low = lax.dot_general(normed, down, nt, preferred_element_type=f32)
    lane = lax.broadcasted_iota(jnp.int32, (rows, base), 1)
    low = jnp.where(lane // rank == seg_low, low, 0.0).astype(bf16)
    own_q = own_q + jnp.dot(low, upsel[c], preferred_element_type=f32)
    q_s[:, cols] = own_q.astype(bf16)

    ones = allowed.astype(f32).astype(bf16)
    levels, levels_t, mixes = [], [], []
    for b in range(2):
        terms = lax.dot_general(normed, gates[b], nt, preferred_element_type=f32)
        shifted = terms + biasr[b][0:1, :]
        log_keep = jnp.minimum(shifted, 0.0) - jnp.log1p(jnp.exp(-jnp.abs(shifted)))
        mixes.append(1.0 / (1.0 + jnp.exp(-terms)))
        part = log_keep.astype(bf16)
        level = jnp.dot(ones, part, preferred_element_type=f32)
        rest = log_keep - part.astype(f32)
        part = rest.astype(bf16)
        level = level + jnp.dot(ones, part, preferred_element_type=f32)
        part = (rest - part.astype(f32)).astype(bf16)
        level = level + jnp.dot(ones, part, preferred_element_type=f32)
        levels.append(level)
        levels_t.append(jnp.transpose(level))

    def index_wait(k, carry):
        q = lax.rem(place + k, nh)
        index_copy(q, q).wait_recv()
        return carry

    def pick(t, q):
        for b in range(2):
            for j in range(seqs):
                i = idxs[q, 0, b * seqs + j]
                piece = r1[t][jnp.minimum(i, own * n - 1)]
                stage[t, q, b, j] = jnp.where(i < own * n, piece, jnp.zeros_like(piece))

    def second_copy(t, q, core, slot, at):
        return pltpu.make_async_remote_copy(
            src_ref=stage.at[t, q, core], dst_ref=r2.at[t, slot, at],
            send_sem=s2.at[(t * nh + q) * 2 + core], recv_sem=t2.at[(t * 2 + slot) * nh + at],
            device_id=(start + q, core), device_id_type=MESH)

    def second_step(t):
        local_c[t].wait()

        def first_wait(k, carry):
            p = lax.rem(g + k, n)
            cache_copy(t, p, p).wait_recv()
            return carry

        lax.fori_loop(1, n, first_wait, 0)

        def second(k, carry):
            q = lax.rem(place + k, nh)
            pick(t, q)
            second_copy(t, q, c, 0, place).start()
            second_copy(t, q, other, 1, place).start()
            return carry

        lax.fori_loop(1, nh, second, 0)
        pick(t, place)
        second_copy(t, place, other, 1, place).start()
        return local(stage.at[t, place, c], r2.at[t, 0, place], 6 + t)

    def second_wait(t):
        def one(k, carry):
            q = lax.rem(place + k, nh)
            second_copy(t, q, c, 0, q).wait_recv()
            second_copy(t, q, other, 1, q).wait_recv()
            return carry

        lax.fori_loop(1, nh, one, 0)
        second_copy(t, place, other, 1, place).wait_recv()
        keep[t].wait()

    lax.fori_loop(1, nh, index_wait, 0)
    local(idxb, idxs, 2).wait()
    keep = [second_step(0)]

    scale = 1.0 / math.sqrt(dh)

    def attend(h):
        cols = pl.ds(h * dh, dh)
        b, i = h // half, h % half
        scores = lax.dot_general(q_s[:, cols], k_s[:, cols], nt, preferred_element_type=f32) * scale
        masked = jnp.where(allowed, scores, -jnp.inf)
        peak = jnp.max(masked, axis=1, keepdims=True)
        weights = jnp.exp(masked - peak)
        probs = (weights * (1.0 / jnp.sum(weights, axis=1, keepdims=True))).astype(bf16)
        att_s[:, cols] = jnp.dot(probs, v_s[:, cols], preferred_element_type=f32)
        gap = jnp.where(allowed, levels[b][:, i:i + 1] - levels_t[b][i:i + 1, :], -jnp.inf)
        memory_w = (scores * jnp.exp(gap)).astype(bf16)
        intra_s[:, cols] = jnp.dot(memory_w, v_s[:, cols], preferred_element_type=f32)

    for h in range(half):
        attend(h)
    pair_w.wait_recv()
    cols = pl.ds(width, width)
    q = jnp.dot(normed, wq[1, 0], preferred_element_type=f32)
    q_s[:, cols] = (q + jnp.dot(low, upr[...], preferred_element_type=f32)).astype(bf16)
    k_s[:, cols] = jnp.dot(normed, wq[1, 1], preferred_element_type=f32).astype(bf16)
    v_s[:, cols] = jnp.dot(normed, wq[1, 2], preferred_element_type=f32).astype(bf16)
    keep.append(second_step(1))
    for h in range(half, 2 * half):
        attend(h)

    per_head = 2 * nh // half

    def recall(b, i):
        h = b * half + i
        t, at = i // (half // 2), (i % (half // 2)) * per_head
        cols = pl.ds(h * dh, dh)
        q = q_s[:, cols]
        carried = jnp.zeros((rows, dh), f32)
        for j in range(seqs):
            state = r2[t, b, at:at + per_head, j]
            state = state.astype(f32).reshape(dh, dh).astype(bf16)
            carried = jnp.where(seg_wide == j, jnp.dot(q, state, preferred_element_type=f32), carried)
        recalled = carried * jnp.exp(levels[b][:, i:i + 1]) + intra_s[:, cols]
        factor = lax.rsqrt(jnp.mean(recalled * recalled, axis=1, keepdims=True) + epsilon)
        head_s[:, cols] = (att_s[:, cols] + mixes[b][:, half + i:half + i + 1] * recalled * factor).astype(bf16)

    local_wo.wait()
    pair_wo.wait_recv()
    mid = width // 2
    proj = tok_ref[...].astype(f32)
    for t in range(2):
        second_wait(t)
        for b in range(2):
            for i in range(t * (half // 2), (t + 1) * (half // 2)):
                recall(b, i)
        for b in range(2):
            at = b * width + t * mid
            proj = proj + jnp.dot(
                head_s[:, at:at + mid], wo[b, t * mid:(t + 1) * mid, :], preferred_element_type=f32)
    mixed = proj.astype(bf16).astype(f32)
    factor = lax.rsqrt(jnp.mean(mixed * mixed, axis=-1, keepdims=True) + epsilon)
    normed_two = (mixed * factor * gain_ref[1:2, :]).astype(bf16)
    local_ff.wait()
    for b in range(2):
        if b == 1:
            pair_ff[0].wait_recv()
        gate = jnp.dot(normed_two, wff[b, 0], preferred_element_type=f32)
        if b == 1:
            pair_ff[1].wait_recv()
        upper = jnp.dot(normed_two, wff[b, 1], preferred_element_type=f32)
        hidden = (gate / (1.0 + jnp.exp(-gate)) * upper).astype(bf16)
        if b == 1:
            pair_ff[2].wait_recv()
        down_t = lax.dot_general(wff[b, 2], hidden, nt, preferred_element_type=f32)
        feed_t = down_t if b == 0 else feed_t + down_t
    out_ref[...] = (mixed + jnp.transpose(feed_t)).astype(bf16)

    def drain_first(k, carry):
        p = lax.rem(g + k, n)
        cache_copy(0, p, g).wait_send()
        cache_copy(1, p, g).wait_send()
        return carry

    def drain_second(k, carry):
        q = lax.rem(place + k, nh)
        index_copy(q, place).wait_send()
        for t in range(2):
            second_copy(t, q, c, 0, place).wait_send()
            second_copy(t, q, other, 1, place).wait_send()
        return carry

    lax.fori_loop(1, n, drain_first, 0)
    lax.fori_loop(1, nh, drain_second, 0)
    for t in range(2):
        second_copy(t, place, other, 1, place).wait_send()
    for one in pairs:
        one.wait_send()


def on_device(
    tokens, norm_gain_pair, query_key_value_weight, head_gate_weight, decay_logit_bias,
    adapter_down_factor, adapter_up_factor, lengths, request_adapter_index, request_cache_index,
    caches, head_output_weight, feedforward_weight,
):
    n = lax.axis_size("req")
    rows, width = tokens.shape
    seqs = lengths.shape[2]
    adapters, _, rank = adapter_down_factor.shape
    half = head_gate_weight.shape[2]
    head_cols = query_key_value_weight.shape[2]
    dh = head_cols // half
    own = caches.shape[0]
    nh = n // 2
    piece = half * dh // n
    base = seqs * rank
    bf16, f32 = jnp.bfloat16, jnp.float32

    vmem = pl.BlockSpec(memory_space=pltpu.VMEM)
    smem = pl.BlockSpec(memory_space=pltpu.SMEM)
    hbm = pl.BlockSpec(memory_space=pl.ANY)
    dma = pltpu.SemaphoreType.DMA
    wide = 2 * head_cols
    return pl.pallas_call(
        functools.partial(mix_kernel, n, seqs, rank, half, dh),
        out_shape=jax.ShapeDtypeStruct((rows, width), bf16),
        in_specs=[smem] * 4 + [vmem] * 3 + [hbm] * 6,
        out_specs=vmem,
        scratch_shapes=[
            pltpu.VMEM((adapters, rank, width), bf16),
            pltpu.VMEM(adapter_up_factor.shape, bf16),
            pltpu.VMEM((2, base, width), bf16),
            pltpu.VMEM((base, width), bf16),
            pltpu.VMEM((2, base, head_cols), bf16),
            pltpu.VMEM((base, head_cols), bf16),
            pltpu.VMEM((2, 8, 128), f32),
            pltpu.VMEM((2, 128, width), bf16),
            pltpu.VMEM((2,) + query_key_value_weight.shape, bf16),
            pltpu.VMEM((2,) + head_output_weight.shape, bf16),
            pltpu.VMEM((2,) + feedforward_weight.shape, bf16),
            pltpu.VMEM((own * n, piece, dh), bf16),
            pltpu.VMEM((own * n, piece, dh), bf16),
            pltpu.VMEM((nh, 8, 128), jnp.int32),
            pltpu.SMEM((nh, 8, 128), jnp.int32),
            pltpu.VMEM((2, nh, 2, seqs, piece, dh), bf16),
            pltpu.VMEM((2, 2, nh, seqs, piece, dh), bf16),
            pltpu.VMEM((rows, wide), bf16),
            pltpu.VMEM((rows, wide), bf16),
            pltpu.VMEM((rows, wide), bf16),
            pltpu.VMEM((rows, wide), f32),
            pltpu.VMEM((rows, wide), f32),
            pltpu.VMEM((rows, wide), bf16),
            dma((2 * n,)), dma((2 * n,)), dma((nh,)), dma((nh,)), dma((4 * nh,)), dma((4 * nh,)),
            dma((10,)), dma((10,)), dma((10,)),
        ],
        compiler_params=pltpu.CompilerParams(
            collective_id=0, has_side_effects=True, vmem_limit_bytes=56 * 2**20),
        cost_estimate=pl.CostEstimate(flops=7 * 10**9, bytes_accessed=3 * 10**7, transcendentals=10**6),
    )(
        lengths, request_adapter_index, request_cache_index, decay_logit_bias, tokens, norm_gain_pair,
        head_gate_weight.transpose(0, 2, 1), adapter_down_factor.transpose(0, 2, 1), adapter_up_factor, query_key_value_weight,
        caches.reshape(own, 2, nh, piece, dh), head_output_weight, feedforward_weight,
    )


def solution(mesh):
    placed = (
        P(("req", "col"), None),
        P(),
        P(None, None, "col"),
        P(None, None, "col"),
        P("col"),
        P("col", None, None),
        P(None, None, "col"),
        P("req", None, None),
        P("req", None),
        P("req", None),
        P("req", "col", None, None),
        P("col", None),
        P(None, None, "col"),
    )
    return jax.shard_map(
        on_device, mesh=mesh, in_specs=placed, out_specs=P(("req", "col"), None), check_vma=False
    )
```
